32 devices in a mesh: dp: 8 (over y, x, core), tensor: 4 (over z).
Axes of the slice: x: 2, y: 2, z: 4, core: 2. Of those that a mesh axis runs over, the one named last changes fastest.
Arguments:
- tokens: bfloat16 [16384, 1536], P(('dp', 'tensor')), may hold values from -6 to 6
- granularity: int32 [16], P('dp'), may hold values from 0 to 3, as said below
- gain_one: float32 [1536], replicated, may hold values from 0.5 to 1.5
- shift_one: float32 [1536], replicated, may hold values from -1.5 to 1.5
- w_qkv: bfloat16 [3, 1536, 1536], P(None, None, 'tensor'), may hold values from -0.15625 to 0.15625
- w_out: bfloat16 [1536, 1536], P('tensor'), may hold values from -0.625 to 0.625
- gain_two: float32 [1536], replicated, may hold values from 0.5 to 1.5
- shift_two: float32 [1536], replicated, may hold values from -1.5 to 1.5
- w_up: bfloat16 [1536, 6144], P(None, 'tensor'), may hold values from -0.15625 to 0.15625
- w_down: bfloat16 [6144, 1536], P('tensor'), may hold values from -0.15625 to 0.15625
- cotangent: bfloat16 [16384, 1536], P(('dp', 'tensor')), may hold values from -6 to 6
Outputs:
- layer_out: bfloat16 [16384, 1536], P(('dp', 'tensor'))
- grad_tokens: float32 [16384, 1536], P(('dp', 'tensor'))
- grad_gain_one: float32 [1536], replicated
- grad_shift_one: float32 [1536], replicated
- grad_qkv: float32 [3, 1536, 1536], P(None, None, 'tensor')
- grad_out: float32 [1536, 1536], P('tensor')
- grad_gain_two: float32 [1536], replicated
- grad_shift_two: float32 [1536], replicated
- grad_up: float32 [1536, 6144], P(None, 'tensor')
- grad_down: float32 [6144, 1536], P('tensor')
The draws below stay inside these ranges and needn't reach their ends.
Inputs may be any that keep to these rules, and one draw needn't show every extreme that they name: hidden unit j serves the tokens of sequence s when j < 6144 // 8 * 2**granularity[s].
All inputs are finite; a program needn't handle non-finite values.
Results may differ from the reference program's by a relative error of at most 0.015.
Values may be sent and summed in bfloat16 or wider, within the bound.
No kernel may reach another device: no remote copies, remote signals or barrier semaphores. Data moves between devices by JAX's collectives and lax.ppermute only.
A program may use at most 192 MiB of HBM per device.

```python
import math
import jax
import jax.numpy as jnp
from jax import lax

D = 1536
HEADS = 12
HD = 128
FF = 6144
SEQ_LEN = 1024
SEQ_DEV = 2
SEQS = 16
TOKENS = 16384


def draw_granularity(key, part):
    key = jax.random.fold_in(key, 7)
    pick_key, order_key = jax.random.split(key)
    levels = jax.random.randint(pick_key, (SEQS,), 0, 4)
    shuffle = jax.random.permutation(order_key, SEQS)
    levels = levels.at[shuffle[0]].set(0)
    levels = levels.at[shuffle[1]].set(3)
    return levels.astype(jnp.int32)


def block_scale(rng, dims, pieces, least, high):
    factor_of = 1.0
    for axis_at, shards_of in pieces:
        steps = jax.random.uniform(jax.random.fold_in(jax.random.fold_in(rng, 6), axis_at), (shards_of,), jnp.float32, least / len(pieces), high / len(pieces))
        factor_of = factor_of * jnp.repeat(jnp.exp(steps), dims[axis_at] // shards_of).reshape((-1,) + (1,) * (len(dims) - 1 - axis_at))
    return factor_of


def bell_draw(own_key, dims, width, limit, cuts=(), kind=jnp.bfloat16):
    result = width * jax.random.normal(own_key, dims, jnp.float32)
    if cuts:
        result = result * block_scale(own_key, dims, cuts, -0.22, 0.18)
    return jnp.clip(result, -limit, limit).astype(kind)


def setup_inputs(seed: int = 0) -> dict:
    seeds = jax.random.split(jax.random.key(seed), 12)
    tokens = bell_draw(seeds[0], (TOKENS, D), 1.0, 6.0, ((0, 32),))
    granularity = draw_granularity(jax.random.fold_in(seeds[11], 71), 0)
    gain_one = jnp.clip(1.0 + 0.1 * jax.random.normal(seeds[2], (D,), jnp.float32), 0.5, 1.5)
    shift_one = bell_draw(seeds[3], (D,), 0.3, 1.5, (), jnp.float32)
    w_qkv = bell_draw(seeds[4], (3, D, D), D ** -0.5, 0.15625, ((2, 4),))
    w_out = bell_draw(seeds[5], (D, D), (D // 16) ** -0.5, 0.625, ((0, 4),))
    gain_two = jnp.clip(1.0 + 0.1 * jax.random.normal(seeds[6], (D,), jnp.float32), 0.5, 1.5)
    shift_two = bell_draw(seeds[7], (D,), 0.3, 1.5, (), jnp.float32)
    w_up = bell_draw(seeds[8], (D, FF), D ** -0.5, 0.15625, ((1, 4),))
    w_down = bell_draw(seeds[9], (FF, D), (FF // 4) ** -0.5, 0.15625, ((0, 4),))
    cotangent = bell_draw(seeds[10], (TOKENS, D), 1.0, 6.0, ((0, 32),))
    return dict(tokens=tokens, granularity=granularity, gain_one=gain_one, shift_one=shift_one, w_qkv=w_qkv, w_out=w_out, gain_two=gain_two, shift_two=shift_two, w_up=w_up, w_down=w_down, cotangent=cotangent)


@jax.custom_vjp
def low(v):
    return lax.optimization_barrier(v.astype(jnp.bfloat16)).astype(jnp.float32)

@jax.custom_vjp
def low_back(v):
    return v

def low_keep(v):
    return (low(v), None)

def low_pass(kept, grad):
    return (grad,)

def back_keep(v):
    return (v, None)

def back_low(kept, grad):
    return (low(grad),)
low.defvjp(low_keep, low_pass)
low_back.defvjp(back_keep, back_low)

def norm_apply(values, gain, shift):
    center = values - lax.optimization_barrier(jnp.mean(values, axis=-1, keepdims=True))
    spread = lax.optimization_barrier(jnp.mean(center * center, axis=-1, keepdims=True))
    return center * lax.rsqrt(spread + 1e-05) * gain + shift

def rope_tables(length, head_dim):
    half_dim = head_dim // 2
    frequency = jnp.exp(jnp.arange(half_dim, dtype=jnp.float32) * (-2.0 * math.log(10000.0) / head_dim))
    angles = jnp.arange(length, dtype=jnp.float32)[:, None] * frequency[None, :]
    return (jnp.cos(angles)[:, None, :], jnp.sin(angles)[:, None, :])

def rotate(values, cos_part, sin_part):
    half_dim = values.shape[-1] // 2
    low_half = values[..., :half_dim]
    high_half = values[..., half_dim:]
    return jnp.concatenate([low_half * cos_part - high_half * sin_part, high_half * cos_part + low_half * sin_part], axis=-1)

def attend(members):
    queries, key_rows, value_rows = members
    length = queries.shape[0]
    raw_scores = low_back(jnp.einsum('qhd,khd->hqk', queries, key_rows, precision=lax.Precision.HIGHEST))
    scores = raw_scores * HD ** (-0.5)
    row_place = lax.broadcasted_iota(jnp.int32, (length, length), 0)
    col_place = lax.broadcasted_iota(jnp.int32, (length, length), 1)
    scores = jnp.where((row_place >= col_place)[None], scores, -1e+30)
    attn_probs = jax.nn.softmax(scores, axis=-1)
    return jnp.einsum('hqk,khd->qhd', low(attn_probs), value_rows, precision=lax.Precision.HIGHEST)

def block_forward(values, granularity, gain_one, shift_one, w_qkv, w_out, gain_two, shift_two, w_up, w_down):
    row_total = SEQ_DEV * SEQ_LEN
    normed_one = low(norm_apply(values, gain_one, shift_one))
    projected = low_back(jnp.einsum('rd,cde->cre', normed_one, w_qkv, precision=lax.Precision.HIGHEST))
    projected = projected.reshape(3, SEQ_DEV, SEQ_LEN, HEADS, HD)
    cos_part, sin_part = rope_tables(SEQ_LEN, HD)
    queries = low(rotate(projected[0], cos_part, sin_part))
    key_rows = low(rotate(projected[1], cos_part, sin_part))
    value_rows = low(projected[2])
    attended = lax.map(jax.checkpoint(attend), (queries, key_rows, value_rows))
    attended = low(low_back(attended.reshape(row_total, D)))
    resid = values + low_back(jnp.dot(attended, w_out, preferred_element_type=jnp.float32, precision=lax.Precision.HIGHEST))
    normed_two = low(norm_apply(resid, gain_two, shift_two))
    pre_act = low_back(jnp.dot(normed_two, w_up, preferred_element_type=jnp.float32, precision=lax.Precision.HIGHEST))
    pre_act = pre_act.reshape(SEQ_DEV, SEQ_LEN, FF)
    unit_limit = jnp.left_shift(jnp.ones_like(granularity), granularity) * (FF // 8)
    unit_index = jnp.arange(FF, dtype=jnp.int32)
    unit_mask = (unit_index[None, :] < unit_limit[:, None]).astype(jnp.float32)[:, None, :]
    hidden = low(jax.nn.gelu(pre_act, approximate=True) * unit_mask).reshape(row_total, FF)
    down_rows = low_back(jnp.dot(hidden, w_down, preferred_element_type=jnp.float32, precision=lax.Precision.HIGHEST))
    return resid + down_rows

def reference(tokens, granularity, gain_one, shift_one, w_qkv, w_out, gain_two, shift_two, w_up, w_down, cotangent):
    params = tuple((item.astype(jnp.float32) for item in (gain_one, shift_one, w_qkv, w_out, gain_two, shift_two, w_up, w_down)))
    row_total = SEQ_DEV * SEQ_LEN
    blocks = tokens.shape[0] // row_total
    token_blocks = tokens.astype(jnp.float32).reshape(blocks, row_total, D)
    grad_blocks = cotangent.astype(jnp.float32).reshape(blocks, row_total, D)
    level_blocks = granularity.reshape(blocks, SEQ_DEV)

    def step_block(totals, members):
        block_tokens, block_levels, block_grad = members

        def forward_only(values, *weights):
            return block_forward(values, block_levels, *weights)
        output, pull = jax.vjp(forward_only, block_tokens, *params)
        grads = pull(block_grad)
        new_totals = tuple((total + grad for total, grad in zip(totals, grads[1:])))
        return (new_totals, (output.astype(jnp.bfloat16), grads[0]))
    start_totals = tuple((jnp.zeros(item.shape, jnp.float32) for item in params))
    totals, (outputs, grad_rows) = lax.scan(step_block, start_totals, (token_blocks, level_blocks, grad_blocks))
    layer_out = outputs.reshape(tokens.shape[0], D)
    grad_tokens = grad_rows.reshape(tokens.shape[0], D)
    return (layer_out, grad_tokens, totals[0], totals[1], totals[2], totals[3], totals[4], totals[5], totals[6], totals[7])
```

```python
import functools
import math

import jax
import jax.numpy as jnp
from jax import lax
from jax.experimental import pallas as pl
from jax.experimental.pallas import tpu as pltpu
from jax.sharding import PartitionSpec as P

HD = 128
FF = 6144
EPS = 1e-05
AXES = ("dp", "tensor")
BF = jnp.bfloat16
F32 = jnp.float32
LOG2E = 1.4426950408889634
VMEM_LIMIT = 56 * 1024 * 1024


def swap(value, dp_bits, tensor_bits):
    dp_size = lax.axis_size("dp")
    tensor_size = lax.axis_size("tensor")
    pairs = [
        (d * tensor_size + t, (d ^ dp_bits) * tensor_size + (t ^ tensor_bits))
        for d in range(dp_size)
        for t in range(tensor_size)
    ]
    return lax.ppermute(value, AXES, pairs)


def fetch(weight):
    dp_size = lax.axis_size("dp")
    rows = weight.shape[0] // dp_size
    piece = lax.dynamic_slice_in_dim(weight, lax.axis_index("dp") * rows, rows, 0)
    return lax.all_gather(swap(piece, 0, 2), "dp", axis=0, tiled=True)


def scatter_step(value, bit):
    side = (lax.axis_index("dp") >> bit) & 1
    rows = value.shape[1] // 2
    keep = lax.dynamic_slice_in_dim(value, side * rows, rows, 1)
    send = lax.dynamic_slice_in_dim(value, (1 - side) * rows, rows, 1)
    return (keep.astype(F32) + swap(send, 1 << bit, 0).astype(F32)).astype(BF)


def settle(pair, order):
    for bit in order:
        pair = scatter_step(pair, bit)
    piece = (pair[0].astype(F32) + swap(pair[1], 0, 2).astype(F32)).astype(BF)
    whole = lax.all_gather(piece, "dp", axis=0, tiled=True)
    count = len(order)
    blocks = whole.reshape((2,) * count + piece.shape)
    axes = [count - 1 - bit for bit in order] + [count, count + 1]
    return blocks.transpose(axes).reshape(whole.shape).astype(F32)


def rope_tables(length):
    half_dim = HD // 2
    frequency = jnp.exp(
        jnp.arange(half_dim, dtype=F32) * (-2.0 * math.log(10000.0) / HD)
    )
    angles = jnp.arange(length, dtype=F32)[:, None] * frequency[None, :]
    cos_part, sin_part = jnp.cos(angles), jnp.sin(angles)
    return (
        jnp.concatenate([cos_part, cos_part], axis=1),
        jnp.concatenate([-sin_part, sin_part], axis=1),
    )


def project_body(x_ref, w_ref, cos_ref, sin_ref, out_ref):
    result = jnp.dot(x_ref[...], w_ref[0], preferred_element_type=F32)
    which = pl.program_id(0)

    @pl.when(which < 2)
    def _():
        for h in range(result.shape[1] // HD):
            part = result[:, h * HD : (h + 1) * HD]
            turned = part * cos_ref[...] + pltpu.roll(part, HD // 2, 1) * sin_ref[...]
            out_ref[0, :, h * HD : (h + 1) * HD] = turned.astype(BF)

    @pl.when(which == 2)
    def _():
        out_ref[0] = result.astype(BF)


def project(rows, weight, tables):
    length, depth = rows.shape
    width = weight.shape[2]
    return pl.pallas_call(
        project_body,
        grid=(3,),
        in_specs=[
            pl.BlockSpec((length, depth), lambda c: (0, 0)),
            pl.BlockSpec((1, depth, width), lambda c: (c, 0, 0)),
            pl.BlockSpec((length, HD), lambda c: (0, 0)),
            pl.BlockSpec((length, HD), lambda c: (0, 0)),
        ],
        out_specs=pl.BlockSpec((1, length, width), lambda c: (c, 0, 0)),
        out_shape=jax.ShapeDtypeStruct((3, length, width), BF),
        compiler_params=pltpu.CompilerParams(vmem_limit_bytes=VMEM_LIMIT),
        cost_estimate=pl.CostEstimate(
            flops=6 * length * depth * width,
            bytes_accessed=2 * (length * depth + 3 * depth * width + 3 * length * width),
            transcendentals=0,
        ),
    )(rows, weight, *tables)


QB = 256
NT = (((1,), (1,)), ((), ()))
TN = (((0,), (0,)), ((), ()))


def mm(a, b, dims=(((1,), (0,)), ((), ()))):
    return lax.dot_general(a, b, dims, preferred_element_type=F32)


def probs_t(q, k, first):
    scores = mm(k, q, NT)
    size = scores.shape[0]
    key_at = lax.broadcasted_iota(jnp.int32, scores.shape, 0)
    row_at = lax.broadcasted_iota(jnp.int32, scores.shape, 1) + first
    scores = jnp.where(key_at <= row_at, scores, -1e30)
    top = jnp.max(scores, axis=0, keepdims=True)
    scale = HD ** (-0.5) * LOG2E
    weights = jnp.exp2((scores - top) * scale)
    total = jnp.sum(weights, axis=0, keepdims=True)
    return weights, 1.0 / total


def attend_body(q_ref, k_ref, v_ref, out_ref):
    length = q_ref.shape[1]
    for first in range(0, length, QB):
        last = first + QB
        q = q_ref[0, first:last]
        weights, inverse = probs_t(q, k_ref[0, :last], first)
        blended = mm(v_ref[0, :last], (weights * inverse).astype(BF), TN)
        out_ref[first:last, :] = blended.T.astype(BF)


def attend(qkv):
    _, length, width = qkv.shape
    heads = width // HD
    spec = lambda c: pl.BlockSpec((1, length, HD), lambda h: (c, 0, h))
    return pl.pallas_call(
        attend_body,
        grid=(heads,),
        in_specs=[spec(0), spec(1), spec(2)],
        out_specs=pl.BlockSpec((length, HD), lambda h: (0, h)),
        out_shape=jax.ShapeDtypeStruct((length, width), BF),
        compiler_params=pltpu.CompilerParams(vmem_limit_bytes=VMEM_LIMIT),
        cost_estimate=pl.CostEstimate(
            flops=8 * length * length * width,
            bytes_accessed=8 * length * width,
            transcendentals=heads * length * length,
        ),
    )(qkv, qkv, qkv)


def back_body(q_ref, k_ref, v_ref, g_ref, cos_ref, sin_ref, out_ref, dk_ref, dv_ref):
    length = q_ref.shape[1]

    def unturn(grads, cos_part, sin_part):
        return (grads * cos_part - pltpu.roll(grads, HD // 2, 1) * sin_part).astype(BF)

    for first in reversed(range(0, length, QB)):
        last = first + QB
        q = q_ref[0, first:last]
        g = g_ref[first:last]
        k = k_ref[0, :last]
        v = v_ref[0, :last]
        weights, inverse = probs_t(q, k, first)
        probs = weights * inverse
        grad_probs = mm(v, g, NT)
        inner = jnp.sum(probs * grad_probs, axis=0, keepdims=True)
        grad_scores = (probs * (grad_probs - inner) * HD ** (-0.5)).astype(BF)
        grad_v = mm(probs.astype(BF), g)
        grad_k = mm(grad_scores, q)
        if last == length:
            dv_ref[...] = grad_v
            dk_ref[...] = grad_k
        else:
            dv_ref[:last] += grad_v
            dk_ref[:last] += grad_k
        grad_q = mm(grad_scores, k, TN)
        out_ref[0, first:last] = unturn(grad_q, cos_ref[first:last], sin_ref[first:last])
    out_ref[1] = unturn(dk_ref[...], cos_ref[...], sin_ref[...])
    out_ref[2] = dv_ref[...].astype(BF)


def attend_back(qkv, grads, tables):
    _, length, width = qkv.shape
    heads = width // HD
    spec = lambda c: pl.BlockSpec((1, length, HD), lambda h: (c, 0, h))
    table = pl.BlockSpec((length, HD), lambda h: (0, 0))
    return pl.pallas_call(
        back_body,
        grid=(heads,),
        in_specs=[
            spec(0),
            spec(1),
            spec(2),
            pl.BlockSpec((length, HD), lambda h: (0, h)),
            table,
            table,
        ],
        out_specs=pl.BlockSpec((3, length, HD), lambda h: (0, 0, h)),
        out_shape=jax.ShapeDtypeStruct((3, length, width), BF),
        scratch_shapes=[pltpu.VMEM((length, HD), F32), pltpu.VMEM((length, HD), F32)],
        compiler_params=pltpu.CompilerParams(vmem_limit_bytes=VMEM_LIMIT),
        cost_estimate=pl.CostEstimate(
            flops=20 * length * length * width,
            bytes_accessed=14 * length * width,
            transcendentals=heads * length * length,
        ),
    )(qkv, qkv, qkv, grads, *tables)


def norm_stats(values):
    center = values - jnp.mean(values, axis=-1, keepdims=True)
    spread = jnp.mean(center * center, axis=-1, keepdims=True)
    inverse = lax.rsqrt(spread + EPS)
    return center * inverse, inverse


def norm_back(grads, normal, inverse, gain):
    scaled = grads * gain
    mean_one = jnp.mean(scaled, axis=-1, keepdims=True)
    mean_two = jnp.mean(scaled * normal, axis=-1, keepdims=True)
    return (
        inverse * (scaled - mean_one - normal * mean_two),
        jnp.sum(grads * normal, axis=0),
        jnp.sum(grads, axis=0),
    )


def gelu_pair(v):
    c = math.sqrt(2.0 / math.pi)
    square = v * v
    t = jnp.tanh(c * v * (1.0 + 0.044715 * square))
    half = 0.5 * (1.0 + t)
    slope = half + 0.5 * v * (1.0 - t * t) * (c * (1.0 + 3.0 * 0.044715 * square))
    return v * half, slope


def shards(
    tokens,
    granularity,
    gain_one,
    shift_one,
    w_qkv,
    w_out,
    gain_two,
    shift_two,
    w_up,
    w_down,
    cotangent,
):
    tensor_size = lax.axis_size("tensor")
    dp_size = lax.axis_size("dp")
    rank = lax.axis_index("tensor")
    local_rows, depth = tokens.shape
    seq_len = local_rows * tensor_size // granularity.shape[0]
    assert tensor_size == 4 and seq_len == 2 * local_rows
    half = local_rows // 2
    hidden_here = w_up.shape[1]
    head_width = w_qkv.shape[2]
    odd = rank % 2
    tables = rope_tables(seq_len)
    dp_bits = [b for b in range(dp_size.bit_length() - 1)]
    other_bits = [0, 2, 1] + dp_bits[3:]

    def in_place(own, other):
        return jnp.where(
            odd == 0,
            jnp.concatenate([own, other], axis=0),
            jnp.concatenate([other, own], axis=0),
        )

    def own_rows(full):
        return lax.dynamic_slice_in_dim(full, odd * local_rows, local_rows, 0)

    def partner_rows(full):
        return lax.dynamic_slice_in_dim(full, (1 - odd) * local_rows, local_rows, 0)

    tokens_wide = tokens.astype(F32)
    normal_one, inverse_one = norm_stats(tokens_wide)
    normed_one = (normal_one * gain_one + shift_one).astype(BF)
    rows_one = in_place(normed_one, swap(normed_one, 0, 1))

    w_qkv_far = fetch(w_qkv.reshape(3 * depth, head_width)).reshape(w_qkv.shape)
    w_out_far = fetch(w_out)
    w_up_far = fetch(w_up)
    w_down_far = fetch(w_down)
    grad_rows = jnp.concatenate(
        [cotangent, swap(cotangent[:half], 0, 1), swap(cotangent[half:], 0, 3)], axis=0
    )

    qkv_near = project(rows_one, w_qkv, tables)
    att_near = attend(qkv_near)
    qkv_far = project(rows_one, w_qkv_far, tables)
    att_far = attend(qkv_far)

    def out_rows(pick):
        return mm(pick(att_near), w_out) + mm(pick(att_far), w_out_far)

    leaving = out_rows(partner_rows).astype(BF)
    arrived_b = swap(leaving[half:], 0, 1)
    arrived_a = swap(leaving[:half], 0, 1)
    staying = out_rows(own_rows)
    resid = tokens_wide + staying + jnp.concatenate([arrived_a, arrived_b], axis=0).astype(F32)

    normal_two, inverse_two = norm_stats(resid)
    normed_two = (normal_two * gain_two + shift_two).astype(BF)
    rows_two = jnp.concatenate(
        [normed_two, swap(normed_two[:half], 0, 1), swap(normed_two[half:], 0, 3)], axis=0
    )
    limits = jnp.left_shift(jnp.ones_like(granularity), granularity) * (FF // 8)
    near_limit = jnp.where(rank < 2, limits[0], limits[1])
    away_limit = jnp.where(rank < 2, limits[1], limits[0])
    row_limit = jnp.where(jnp.arange(4 * half) < 3 * half, near_limit, away_limit)[:, None]
    unit = jnp.arange(hidden_here, dtype=jnp.int32)[None, :]

    def feed(w_up_one, w_down_one, place):
        mask = (unit + place * hidden_here < row_limit).astype(F32)
        value, slope = gelu_pair(mm(rows_two, w_up_one))
        grad_hidden = mm(grad_rows, w_down_one, NT)
        return (value * mask).astype(BF), (grad_hidden * mask * slope).astype(BF)

    hidden_near, pre_near = feed(w_up, w_down, rank)
    hidden_far, pre_far = feed(w_up_far, w_down_far, rank ^ 2)

    def back_two(lo, hi):
        return mm(pre_near[lo:hi], w_up, NT) + mm(pre_far[lo:hi], w_up_far, NT)

    def down(lo, hi):
        return mm(hidden_near[lo:hi], w_down) + mm(hidden_far[lo:hi], w_down_far)

    leave_two = back_two(2 * half, 4 * half).astype(BF)
    back_a = swap(leave_two[:half], 0, 1)
    back_b = swap(leave_two[half:], 0, 3)
    grad_two = back_two(0, 2 * half) + jnp.concatenate([back_a, back_b], axis=0).astype(F32)
    grad_resid, grad_gain_two, grad_shift_two = norm_back(
        grad_two, normal_two, inverse_two, gain_two
    )
    grad_resid = grad_resid + cotangent.astype(F32)
    grad_low = grad_resid.astype(BF)
    grad_full = in_place(grad_low, swap(grad_low, 0, 1))

    leave_out = down(2 * half, 4 * half).astype(BF)
    down_a = swap(leave_out[:half], 0, 1)
    down_b = swap(leave_out[half:], 0, 3)
    layer_out = resid + down(0, 2 * half) + jnp.concatenate([down_a, down_b], axis=0).astype(F32)
    layer_out = layer_out.astype(BF)

    up_pair = jnp.stack(
        [mm(rows_two, pre_near, TN).astype(BF), mm(rows_two, pre_far, TN).astype(BF)]
    )
    down_pair = jnp.stack(
        [mm(hidden_near, grad_rows, TN).astype(BF), mm(hidden_far, grad_rows, TN).astype(BF)]
    )
    grad_up = settle(up_pair, dp_bits)
    grad_down = settle(down_pair, other_bits)

    grad_att_near = mm(grad_full, w_out, NT).astype(BF)
    grad_att_far = mm(grad_full, w_out_far, NT).astype(BF)
    out_pair = jnp.stack(
        [mm(att_near, grad_full, TN).astype(BF), mm(att_far, grad_full, TN).astype(BF)]
    )
    grad_out = settle(out_pair, dp_bits)
    proj_near = attend_back(qkv_near, grad_att_near, tables)
    proj_far = attend_back(qkv_far, grad_att_far, tables)

    def back_one(offset):
        total = 0.0
        for proj, weight in ((proj_near, w_qkv), (proj_far, w_qkv_far)):
            for c in range(3):
                part = lax.dynamic_slice_in_dim(proj[c], offset, local_rows, 0)
                total = total + mm(part, weight[c], NT)
        return total

    leave_one = back_one((1 - odd) * local_rows).astype(BF)
    back_arrived = swap(leave_one, 0, 1)
    grad_one = back_one(odd * local_rows) + back_arrived.astype(F32)
    grad_local, grad_gain_one, grad_shift_one = norm_back(
        grad_one, normal_one, inverse_one, gain_one
    )
    grad_tokens = grad_resid + grad_local

    def qkv_grad(proj):
        return jnp.concatenate([mm(rows_one, proj[c], TN).astype(BF) for c in range(3)], axis=0)

    qkv_pair = jnp.stack([qkv_grad(proj_near), qkv_grad(proj_far)])
    grad_qkv = settle(qkv_pair, dp_bits).reshape(w_qkv.shape)

    gain_sums = lax.psum(
        jnp.stack([grad_gain_one, grad_shift_one, grad_gain_two, grad_shift_two]), AXES
    )
    return (
        layer_out,
        grad_tokens,
        gain_sums[0],
        gain_sums[1],
        grad_qkv,
        grad_out,
        gain_sums[2],
        gain_sums[3],
        grad_up,
        grad_down,
    )


def solution(mesh):
    rows = P(AXES, None)
    params = (P(), P(), P(None, None, "tensor"), P("tensor", None))
    wide = (P(None, "tensor"), P("tensor", None))
    return jax.shard_map(
        shards,
        mesh=mesh,
        in_specs=(rows, P("dp")) + params + (P(), P()) + wide + (rows,),
        out_specs=(rows, rows) + params + (P(), P()) + wide,
        check_vma=False,
    )
```

```python
import functools
import math

import jax
import jax.numpy as jnp
import numpy as np
from jax import lax
from jax.experimental import pallas as pl
from jax.experimental.pallas import tpu as pltpu
from jax.sharding import PartitionSpec as P

HD = 128
FF = 6144
EPS = 1e-05
AXES = ("dp", "tensor")
BF = jnp.bfloat16
F32 = jnp.float32
LOG2E = 1.4426950408889634
LONG = 200_000_000_000
VMEM_LIMIT = 56 * 1024 * 1024

ODD, SIDE, LIMIT, NEAR_UNIT, FAR_UNIT = 0, 1, 4, 5, 6

NN = (((1,), (0,)), ((), ()))
NT = (((1,), (1,)), ((), ()))
TN = (((0,), (0,)), ((), ()))


def mm(a, b, dims=NN):
    return lax.dot_general(a, b, dims, preferred_element_type=F32)


def swap(value, dp_bits, tensor_bits):
    dp_size = lax.axis_size("dp")
    tensor_size = lax.axis_size("tensor")
    pairs = [
        (d * tensor_size + t, (d ^ dp_bits) * tensor_size + (t ^ tensor_bits))
        for d in range(dp_size)
        for t in range(tensor_size)
    ]
    return lax.ppermute(value, AXES, pairs)


class Chain:
    def __init__(self):
        self.last = None

    def __call__(self, call, *args):
        if self.last is not None:
            leaves, tree = jax.tree.flatten(args)
            leaves = lax.optimization_barrier(tuple(leaves) + (self.last,))[:-1]
            args = jax.tree.unflatten(tree, leaves)
        out = call(*args)
        self.last = jax.tree.leaves(out)[0]
        return out

    def wait(self, *args):
        return self(lambda *v: v[0] if len(v) == 1 else v, *args)


def dp_piece(weight):
    rows = weight.shape[0] // lax.axis_size("dp")
    return lax.dynamic_slice_in_dim(weight, lax.axis_index("dp") * rows, rows, 0)


def from_all(piece):
    return lax.all_gather(piece, "dp", axis=0, tiled=True)


def block(shape, index=None):
    if index is None:
        return pl.BlockSpec(shape, lambda *_: (0,) * len(shape))
    return pl.BlockSpec(shape, index)


def shape_of(shape, kind=BF):
    return jax.ShapeDtypeStruct(shape, kind)


def kernel(body, grid, ins, outs, shapes, scratch=(), aliases=None, cost=1):
    return pl.pallas_call(
        body,
        grid_spec=pltpu.PrefetchScalarGridSpec(
            num_scalar_prefetch=1,
            grid=grid,
            in_specs=ins,
            out_specs=outs,
            scratch_shapes=list(scratch),
        ),
        out_shape=shapes,
        input_output_aliases=aliases or {},
        compiler_params=pltpu.CompilerParams(vmem_limit_bytes=VMEM_LIMIT),
        cost_estimate=pl.CostEstimate(flops=cost, bytes_accessed=1, transcendentals=0),
    )


def rows_at(start, size):
    return pl.ds(pl.multiple_of(start, size), size)


def norm_stats(values):
    center = values - jnp.mean(values, axis=-1, keepdims=True)
    spread = jnp.mean(center * center, axis=-1, keepdims=True)
    inverse = lax.rsqrt(spread + EPS)
    return center * inverse, inverse


def norm_back(grads, normal, inverse, gain):
    scaled = grads * gain
    mean_one = jnp.mean(scaled, axis=-1, keepdims=True)
    mean_two = jnp.mean(scaled * normal, axis=-1, keepdims=True)
    return (
        inverse * (scaled - mean_one - normal * mean_two),
        jnp.sum(grads * normal, axis=0, keepdims=True),
        jnp.sum(grads, axis=0, keepdims=True),
    )


def first_norm(place, tokens, gain, shift):
    rows, depth = tokens.shape
    half = rows // 2

    def body(_, x, gain, shift, low, high):
        normal, _ = norm_stats(x[...].astype(F32))
        value = (normal * gain[...] + shift[...]).astype(BF)
        pl.when(pl.program_id(0) == 0)(lambda: low.__setitem__(..., value))
        pl.when(pl.program_id(0) == 1)(lambda: high.__setitem__(..., value))

    return kernel(
        body,
        (2,),
        [block((half, depth), lambda i, _: (i, 0))] + [block((1, depth))] * 2,
        [block((half, depth))] * 2,
        [shape_of((half, depth))] * 2,
    )(place, tokens, gain, shift)


def rope_tables(length):
    frequency = np.exp(
        np.arange(HD // 2, dtype=np.float32) * np.float32(-2.0 * math.log(10000.0) / HD)
    ).astype(np.float32)
    angles = (np.arange(length, dtype=np.float32)[:, None] * frequency[None, :]).astype(np.float64)
    cos_part, sin_part = np.cos(angles), np.sin(angles)
    return (
        np.concatenate([cos_part, cos_part], axis=1).astype(np.float32),
        np.concatenate([-sin_part, sin_part], axis=1).astype(np.float32),
    )


def project(place, own, other, weight, tables):
    part, depth = own[0].shape
    width = weight.shape[2]

    def body(p, ol, oh, tl, th, weight, cos, sin, out):
        def go(source):
            x = source[...]
            for c in range(3):
                result = mm(x, weight[c])
                if c == 2:
                    out[c] = result.astype(BF)
                    continue
                for h in range(width // HD):
                    one = result[:, h * HD : (h + 1) * HD]
                    turned = one * cos[...] + pltpu.roll(one, HD // 2, 1) * sin[...]
                    out[c, :, h * HD : (h + 1) * HD] = turned.astype(BF)

        step = pl.program_id(0)
        at = jnp.where(step // 2 == p[ODD], 0, 2) + step % 2
        for i, source in enumerate((ol, oh, tl, th)):
            pl.when(at == i)(functools.partial(go, source))

    table = block((part, HD), lambda i, _: (i, 0))
    return kernel(
        body,
        (4,),
        [block((part, depth))] * 4 + [block((3, depth, width)), table, table],
        block((3, part, width), lambda i, _: (0, i, 0)),
        shape_of((3, 4 * part, width)),
    )(place, *own, *other, weight, *tables)


QB = 256


def probs_t(q, k, first):
    scores = mm(k, q, NT)
    key_at = lax.broadcasted_iota(jnp.int32, scores.shape, 0)
    row_at = lax.broadcasted_iota(jnp.int32, scores.shape, 1) + first
    scores = jnp.where(key_at <= row_at, scores, -1e30)
    top = jnp.max(scores, axis=0, keepdims=True)
    weights = jnp.exp2((scores - top) * (HD ** (-0.5) * LOG2E))
    return weights, 1.0 / jnp.sum(weights, axis=0, keepdims=True)


def attend(place, qkv):
    _, length, width = qkv.shape

    def body(_, q_ref, k_ref, v_ref, out_ref):
        for first in range(0, length, QB):
            last = first + QB
            weights, inverse = probs_t(q_ref[0, first:last], k_ref[0, :last], first)
            blended = mm(v_ref[0, :last], (weights * inverse).astype(BF), TN)
            out_ref[first:last, :] = blended.T.astype(BF)

    spec = lambda c: block((1, length, HD), lambda h, _: (c, 0, h))
    return kernel(
        body,
        (width // HD,),
        [spec(0), spec(1), spec(2)],
        block((length, HD), lambda h, _: (0, h)),
        shape_of((length, width)),
    )(place, qkv, qkv, qkv)


def attend_back(place, cost, qkv, own, other, w_out, tables):
    _, length, width = qkv.shape
    depth = w_out.shape[1]
    part = length // 4

    def unturn(grads, cos, sin):
        return (grads * cos - pltpu.roll(grads, HD // 2, 1) * sin).astype(BF)

    def body(p, q_ref, k_ref, v_ref, ol, oh, tl, th, w_ref, cos, sin, out, g_ref, dk_ref, dv_ref):
        for base, low, high in ((p[ODD] * 2, ol, oh), ((1 - p[ODD]) * 2, tl, th)):
            g_ref[rows_at(base * part, part)] = mm(low[...], w_ref[...], NT).astype(BF)
            g_ref[rows_at((base + 1) * part, part)] = mm(high[...], w_ref[...], NT).astype(BF)
        for first in reversed(range(0, length, QB)):
            last = first + QB
            q = q_ref[0, first:last]
            g = g_ref[first:last]
            k = k_ref[0, :last]
            weights, inverse = probs_t(q, k, first)
            probs = weights * inverse
            grad_probs = mm(v_ref[0, :last], g, NT)
            inner = jnp.sum(probs * grad_probs, axis=0, keepdims=True)
            grad_scores = (probs * (grad_probs - inner) * HD ** (-0.5)).astype(BF)
            grad_v = mm(probs.astype(BF), g)
            grad_k = mm(grad_scores, q)
            if last == length:
                dv_ref[...] = grad_v
                dk_ref[...] = grad_k
            else:
                dv_ref[:last] += grad_v
                dk_ref[:last] += grad_k
            grad_q = mm(grad_scores, k, TN)
            out[0, first:last] = unturn(grad_q, cos[first:last], sin[first:last])
        out[1] = unturn(dk_ref[...], cos[...], sin[...])
        out[2] = dv_ref[...].astype(BF)

    spec = lambda c: block((1, length, HD), lambda h, _: (c, 0, h))
    piece = block((part, depth))
    table = block((length, HD))
    return kernel(
        body,
        (width // HD,),
        [spec(0), spec(1), spec(2)]
        + [piece] * 4
        + [block((HD, depth), lambda h, _: (h, 0)), table, table],
        block((3, length, HD), lambda h, _: (0, 0, h)),
        shape_of((3, length, width)),
        [pltpu.VMEM((length, HD), BF), pltpu.VMEM((length, HD), F32), pltpu.VMEM((length, HD), F32)],
        cost=cost,
    )(place, qkv, qkv, qkv, *own, *other, w_out, *tables)


def head_rows(place, leave, near, far, w_near, w_far):
    length, width = near.shape
    depth = w_near.shape[1]
    half = length // 4
    kind = BF if leave else F32
    cols = depth // 3

    def body(_, near, far, w_near, w_far, low, high):
        total = mm(near[...], w_near[...]) + mm(far[...], w_far[...])
        low[...] = total[:half].astype(kind)
        high[...] = total[half:].astype(kind)

    rows = block((2 * half, width), lambda i, p: (1 - p[ODD] if leave else p[ODD], 0))
    weight = block((width, cols), lambda i, p: (0, i))
    return kernel(
        body,
        (3,),
        [rows, rows, weight, weight],
        [block((half, cols), lambda i, p: (0, i))] * 2,
        [shape_of((half, depth), kind)] * 2,
    )(place, near, far, w_near, w_far)


def second_norm(place, which, stay, tokens, arrived, gain, shift):
    half, depth = stay.shape
    size = half // 2

    def body(_, stay, tokens, arrived, gain, shift, normed, resid):
        total = tokens[...].astype(F32) + stay[...] + arrived[...].astype(F32)
        resid[...] = total
        normal, _ = norm_stats(total)
        normed[...] = (normal * gain[...] + shift[...]).astype(BF)

    piece = block((size, depth), lambda i, _: (i, 0))
    return kernel(
        body,
        (2,),
        [piece, block((size, depth), lambda i, _: (2 * which + i, 0)), piece]
        + [block((1, depth))] * 2,
        [piece] * 2,
        [shape_of((half, depth)), shape_of((half, depth), F32)],
    )(place, stay, tokens, arrived, gain, shift)


def gelu_pair(v):
    c = math.sqrt(2.0 / math.pi)
    square = v * v
    t = jnp.tanh(v * (c + (c * 0.044715) * square))
    half = 0.5 + 0.5 * t
    slope = half + v * (0.5 - 0.5 * t * t) * (c + (3.0 * 0.044715 * c) * square)
    return v * half, slope


UB = 768
SB = 256


def feed(group, place, normed, normed_far, cot, cot_far, weights, kept=()):
    half, depth = normed.shape
    size = 2 * half
    units = weights[0].shape[1]
    near_steps = units // UB

    def body(p, own, other, g_own, g_other, un, dn, uf, df, *refs):
        hn, pn, hf, pf, rows, grads, stay, leave, total = refs[-9:]
        step = pl.program_id(0)

        @pl.when(step == 0)
        def _():
            total[...] = jnp.zeros_like(total)
            rows[:half] = own[...]
            rows[half:] = other[...]
            grads[:half] = g_own[...]
            grads[half:] = g_other[...]

        def work(up, down, hidden, pre):
            for at in range(0, UB, SB):
                there = slice(at, at + SB)
                value, slope = gelu_pair(mm(rows[...], up[:, there]))
                hidden[:, there] = value.astype(BF)
                grad = mm(grads[...], down[there], NT)
                pre[:, there] = (grad * slope).astype(BF)
            total[...] += mm(pre[...], up[...], NT)

        def part(first_unit, up, down, hidden, pre):
            live = first_unit < p[LIMIT]

            @pl.when(live)
            def _():
                work(up, down, hidden, pre)

            @pl.when(jnp.logical_not(live))
            def _():
                hidden[...] = jnp.zeros((size, UB), BF)
                pre[...] = jnp.zeros((size, UB), BF)

        @pl.when(step < near_steps)
        def _():
            part(p[NEAR_UNIT] + step * UB, un, dn, hn, pn)

        @pl.when(step >= near_steps)
        def _():
            part(p[FAR_UNIT] + (step - near_steps) * UB, uf, df, hf, pf)

        @pl.when(step == 2 * near_steps - 1)
        def _():
            stay[...] = total[:half]
            leave[...] = total[half:].astype(BF)

    near = lambda j: jnp.minimum(j, near_steps - 1)
    far = lambda j: jnp.maximum(j - near_steps, 0)
    ups = [block((depth, UB), lambda j, _, at=at: (0, at(j))) for at in (near, far)]
    downs = [block((UB, depth), lambda j, _, at=at: (at(j), 0)) for at in (near, far)]
    wide = [block((size, UB), lambda j, _, at=at: (group, at(j))) for at in (near, far)]
    piece = block((half, depth))
    rows = block((size, depth), lambda j, _: (group, 0))
    return kernel(
        body,
        (2 * near_steps,),
        [piece, piece, block((half, depth), lambda j, _: (1 - group, 0)), piece]
        + [ups[0], downs[0], ups[1], downs[1]]
        + [pl.BlockSpec(memory_space=pl.ANY)] * len(kept),
        [wide[0], wide[0], wide[1], wide[1], rows, rows, piece, piece],
        [shape_of((2 * size, units))] * 4
        + [shape_of((2 * size, depth))] * 2
        + [shape_of((half, depth), F32), shape_of((half, depth))],
        [pltpu.VMEM((size, depth), F32)],
        {9 + i: i for i in range(len(kept))},
    )(place, normed, normed_far, cot, cot_far, *weights, *kept)


def second_back(place, which, resid, stay, arrived, cot, gain):
    half, depth = resid.shape
    size = half // 2

    def body(_, resid, stay, arrived, cot, gain, low, wide, gain_sum, shift_sum):
        normal, inverse = norm_stats(resid[...])
        grad, gains, shifts = norm_back(
            stay[...] + arrived[...].astype(F32), normal, inverse, gain[...]
        )
        grad = grad + cot[...].astype(F32)
        wide[...] = grad
        low[...] = grad.astype(BF)

        @pl.when(pl.program_id(0) == 0)
        def _():
            gain_sum[...] = gains
            shift_sum[...] = shifts

        @pl.when(pl.program_id(0) > 0)
        def _():
            gain_sum[...] += gains
            shift_sum[...] += shifts

    piece = block((size, depth), lambda i, _: (i, 0))
    vector = block((1, depth))
    return kernel(
        body,
        (2,),
        [piece] * 3 + [block((size, depth), lambda i, _: (2 * which + i, 0)), vector],
        [piece, piece, vector, vector],
        [shape_of((half, depth)), shape_of((half, depth), F32)] + [shape_of((1, depth), F32)] * 2,
    )(place, resid, stay, arrived, cot, gain)


def down_rows(place, near, far, w_near, w_far, resid_high, resid_low):
    rows, units = near.shape
    depth = w_near.shape[1]
    half = rows // 4
    cols = depth // 3

    def body(_, near, far, w_near, w_far, resid_high, resid_low, high, low, out_high, out_low):
        for i, (stay, resid, leave) in enumerate(
            ((out_high, resid_high, high), (out_low, resid_low, low))
        ):
            here = slice(2 * i * half, 2 * (i + 1) * half)
            total = mm(near[here], w_near[...]) + mm(far[here], w_far[...])
            stay[...] = total[:half] + resid[...]
            leave[...] = total[half:].astype(BF)

    hidden = block((rows, units))
    weight = block((units, cols), lambda j, _: (0, j))
    piece = block((half, cols), lambda j, _: (0, j))
    return kernel(
        body,
        (3,),
        [hidden, hidden, weight, weight, piece, piece],
        [piece] * 4,
        [shape_of((half, depth))] * 2 + [shape_of((half, depth), F32)] * 2,
    )(place, near, far, w_near, w_far, resid_high, resid_low)


def layer_rows(place, out_low, out_high, low, high):
    half, depth = low.shape

    def body(_, out_low, out_high, low, high, out):
        out[:half] = (out_low[...] + low[...].astype(F32)).astype(BF)
        out[half:] = (out_high[...] + high[...].astype(F32)).astype(BF)

    piece = block((half, depth))
    return kernel(body, (1,), [piece] * 4, block((2 * half, depth)), shape_of((2 * half, depth)))(
        place, out_low, out_high, low, high
    )


def wide_grad(place, bit, lefts, rights, arrived=None):
    rows, width = lefts[0].shape
    depth = rights[0].shape[1]
    half = width // 2
    cols = depth // 3
    last = arrived is not None

    def body(p, l0, l1, r0, r1, *refs):
        turned = refs[-1]
        shard = pl.program_id(0)

        @pl.when(pl.program_id(1) == 0)
        def _():
            pl.when(shard == 0)(lambda: turned.__setitem__(..., l0[...].T))
            pl.when(shard == 1)(lambda: turned.__setitem__(..., l1[...].T))

        def go(right):
            if not last:
                refs[0][0, 0] = mm(turned[...], right[...]).astype(BF)
                return
            for out, side in ((refs[1], p[SIDE + bit]), (refs[2], 1 - p[SIDE + bit])):
                here = rows_at(side * (half // 2), half // 2)
                value = mm(turned[here], right[...]) + refs[0][0, 0, here].astype(F32)
                out[0, 0] = value.astype(BF)

        pl.when(shard == 0)(lambda: go(r0))
        pl.when(shard == 1)(lambda: go(r1))

    side = lambda p: p[SIDE] if last else 1 - p[SIDE]
    left = block((rows, half), lambda s, j, p: (0, side(p)))
    right = lambda shard: block(
        (rows, cols), lambda s, j, p: (0, jnp.where(s == shard, j, 2 * (1 - shard)))
    )
    tall = lambda size: block((1, 1, size, cols), lambda s, j, p: (s, 0, 0, j))
    if last:
        outs = [tall(half // 2)] * 2
        shapes = [shape_of((2, 1, half // 2, depth))] * 2
    else:
        outs, shapes = tall(half), shape_of((2, 1, half, depth))
    return kernel(
        body,
        (2, 3),
        [left, left, right(0), right(1)] + [tall(half)] * last,
        outs,
        shapes,
        [pltpu.VMEM((half, rows), BF)],
    )(place, *lefts, *rights, *([arrived] if last else []))


def narrow_grad(place, bit, first, total, own, other, nears, fars, arrived=None, kept=()):
    rows, depth = own[0].shape
    parts = len(own)
    count, length, width = nears.shape
    half = depth // 2
    last = arrived is not None
    n_out = 2 if last else 1

    def body(p, *refs):
        own, other = refs[:parts], refs[parts : 2 * parts]
        near, far = refs[2 * parts : 2 * parts + 2]
        arrived, outs, turned = refs[2 * parts + 2], refs[-1 - n_out : -1], refs[-1]
        shard = pl.program_id(0)

        @pl.when((shard == 0) & (pl.program_id(1) == 0))
        def _():
            for lefts, base in ((own, p[ODD]), (other, 1 - p[ODD])):
                for i, left in enumerate(lefts):
                    turned[:, rows_at((base * parts + i) * rows, rows)] = left[...].T

        def go(right):
            if not last:
                outs[0][0, 0] = mm(turned[...], right[0]).astype(BF)
                return
            for out, side in ((outs[0], p[SIDE + bit]), (outs[1], 1 - p[SIDE + bit])):
                here = rows_at(side * (half // 2), half // 2)
                value = mm(turned[here], right[0]) + arrived[0, 0, here].astype(F32)
                out[0, 0] = value.astype(BF)

        pl.when(shard == 0)(lambda: go(near))
        pl.when(shard == 1)(lambda: go(far))

    side = lambda p: p[SIDE] if last else 1 - p[SIDE]
    left = block((rows, half), lambda s, c, p: (0, side(p)))
    right = lambda shard: block(
        (1, length, width),
        lambda s, c, p: (jnp.where(s == shard, c, (count - 1) * (1 - shard)), 0, 0),
    )
    tall = lambda size: block((1, 1, size, width), lambda s, c, p: (s, first + c, 0, 0))
    size = half // 2 if last else half
    ins = [left] * (2 * parts) + [right(0), right(1)] + [tall(half)] * last
    return kernel(
        body,
        (2, count),
        ins + [pl.BlockSpec(memory_space=pl.ANY)] * len(kept),
        [tall(size)] * n_out,
        [shape_of((2, total, size, width))] * n_out,
        [pltpu.VMEM((half, length), BF)],
        {1 + len(ins) + i: i for i in range(len(kept))},
    )(place, *own, *other, nears, fars, *([arrived] if last else []), *kept)


def add_split(place, bit, keep, arrived):
    _, count, rows, width = keep.shape
    half = rows // 2

    def body(p, mine, theirs, keep, send):
        here = rows_at(p[SIDE + bit] * half, half)
        there = rows_at((1 - p[SIDE + bit]) * half, half)
        keep[0, 0] = (mine[0, 0, here].astype(F32) + theirs[0, 0, here].astype(F32)).astype(BF)
        send[0, 0] = (mine[0, 0, there].astype(F32) + theirs[0, 0, there].astype(F32)).astype(BF)

    full = block((1, 1, rows, width), lambda s, c, p: (s, c, 0, 0))
    out = block((1, 1, half, width), lambda s, c, p: (s, c, 0, 0))
    return kernel(
        body, (2, count), [full, full], [out, out], [shape_of((2, count, half, width))] * 2
    )(place, keep, arrived)


def add_last(place, keep, arrived):
    _, count, rows, width = keep.shape

    def body(_, mine, theirs, near, far):
        near[...] = (mine[0].astype(F32) + theirs[0].astype(F32)).astype(BF)
        far[...] = (mine[1].astype(F32) + theirs[1].astype(F32)).astype(BF)

    full = block((2, 1, rows, width), lambda c, p: (0, c, 0, 0))
    out = block((1, rows, width), lambda c, p: (c, 0, 0))
    return kernel(
        body, (count,), [full, full], [out, out], [shape_of((count, rows, width))] * 2
    )(place, keep, arrived)


def add_pair(place, near, arrived):
    count, rows, width = near.shape

    def body(_, mine, theirs, out):
        out[...] = (mine[...].astype(F32) + theirs[...].astype(F32)).astype(BF)

    full = block((1, rows, width), lambda c, p: (c, 0, 0))
    return kernel(body, (count,), [full, full], full, shape_of((count, rows, width)))(
        place, near, arrived
    )


def assemble(table, whole):
    size, count, rows, width = whole.shape

    def body(_, piece, out):
        out[...] = piece[0].astype(F32)

    return kernel(
        body,
        (size,),
        [block((1, count, rows, width), lambda j, t: (t[j], 0, 0, 0))],
        block((count, rows, width), lambda j, t: (0, j, 0)),
        shape_of((count, rows * size, width), F32),
    )(table, whole)


def assemble_heads(table, whole):
    size, count, rows, width = whole.shape

    def body(_, piece, out, last):
        out[...] = piece[0, : count - 1].astype(F32)
        last[pl.program_id(0)] = piece[0, count - 1].astype(F32).T

    out, last = kernel(
        body,
        (size,),
        [block((1, count, rows, width), lambda j, t: (t[j], 0, 0, 0))],
        [
            block((count - 1, rows, width), lambda j, t: (0, j, 0)),
            block((size, width, rows)),
        ],
        [shape_of((count - 1, rows * size, width), F32), shape_of((size, width, rows), F32)],
    )(table, whole)
    return out, last.transpose(1, 0, 2).reshape(width, rows * size)


def back_rows(place, leave, near, far, w_near, w_far):
    count, length, width = near.shape
    depth = w_near.shape[1]
    rows = length // 2
    cols = depth // 3
    kind = BF if leave else F32

    def body(_, near, far, w_near, w_far, out):
        for lo in range(0, rows, rows // 2):
            here = slice(lo, lo + rows // 2)
            total = mm(near[0, here], w_near[0], NT)
            for proj, weight, c in [(near, w_near, c) for c in range(1, count)] + [
                (far, w_far, c) for c in range(count)
            ]:
                total = total + mm(proj[c, here], weight[c], NT)
            out[here] = total.astype(kind)

    at = lambda p: 1 - p[ODD] if leave else p[ODD]
    proj = block((count, rows, width), lambda j, p: (0, at(p), 0))
    weight = block((count, cols, width), lambda j, p: (0, j, 0))
    return kernel(
        body,
        (3,),
        [proj, proj, weight, weight],
        block((rows, cols), lambda j, p: (0, j)),
        shape_of((rows, depth), kind),
        cost=1 if leave else LONG,
    )(place, near, far, w_near, w_far)


def first_back(place, tokens, stay, arrived, resid_low, resid_high, gain):
    rows, depth = tokens.shape
    half = rows // 2

    def body(_, tokens, stay, arrived, resid_low, resid_high, gain, out, gain_sum, shift_sum):
        normal, inverse = norm_stats(tokens[...].astype(F32))
        grad, gains, shifts = norm_back(
            stay[...] + arrived[...].astype(F32), normal, inverse, gain[...]
        )

        @pl.when(pl.program_id(0) == 0)
        def _():
            out[...] = grad + resid_low[...]
            gain_sum[...] = gains
            shift_sum[...] = shifts

        @pl.when(pl.program_id(0) == 1)
        def _():
            out[...] = grad + resid_high[...]
            gain_sum[...] += gains
            shift_sum[...] += shifts

    tile = block((half, depth), lambda i, _: (i, 0))
    piece = block((half, depth))
    vector = block((1, depth))
    return kernel(
        body,
        (2,),
        [tile, tile, tile, piece, piece, vector],
        [tile, vector, vector],
        [shape_of((rows, depth), F32)] + [shape_of((1, depth), F32)] * 2,
        cost=LONG,
    )(place, tokens, stay, arrived, resid_low, resid_high, gain)


def shards(
    tokens,
    granularity,
    gain_one,
    shift_one,
    w_qkv,
    w_out,
    gain_two,
    shift_two,
    w_up,
    w_down,
    cotangent,
):
    tensor_size = lax.axis_size("tensor")
    dp_size = lax.axis_size("dp")
    rank = lax.axis_index("tensor")
    dp_at = lax.axis_index("dp")
    local_rows, depth = tokens.shape
    seq_len = local_rows * tensor_size // granularity.shape[0]
    assert tensor_size == 4 and seq_len == 2 * local_rows and dp_size % 8 == 0
    half = local_rows // 2
    hidden_here = w_up.shape[1]
    head_width = w_qkv.shape[2]
    bits = dp_size.bit_length() - 1
    tables = [jnp.asarray(t) for t in rope_tables(seq_len)]
    gain_one, shift_one, gain_two, shift_two = (
        v[None, :] for v in (gain_one, shift_one, gain_two, shift_two)
    )
    limits = jnp.left_shift(jnp.ones_like(granularity), granularity) * (FF // 8)
    upper = rank // 2
    place = jnp.stack(
        [
            rank % 2,
            dp_at & 1,
            (dp_at >> 1) & 1,
            (dp_at >> 2) & 1,
            jnp.where(upper == 0, limits[0], limits[1]),
            rank * hidden_here,
            (rank ^ 2) * hidden_here,
        ]
    ).astype(jnp.int32)
    chain = Chain()
    run = lambda call, *args: chain(functools.partial(call, place), *args)

    piece_qkv = swap(chain(dp_piece, w_qkv.reshape(3 * depth, head_width)), 0, 2)
    normed = run(first_norm, tokens, gain_one, shift_one)
    normed_far = [swap(v, 0, 1) for v in normed]
    normed_far[0], piece_qkv = chain.wait(normed_far[0], piece_qkv)
    w_qkv_far = from_all(piece_qkv).reshape(w_qkv.shape)
    piece_out, piece_up = chain(lambda a, b: (dp_piece(a), dp_piece(b)), w_out, w_up)
    piece_out, piece_up = swap(piece_out, 0, 2), swap(piece_up, 0, 2)
    normed_far[1], piece_out = chain.wait(normed_far[1], piece_out)
    w_out_far = from_all(piece_out)
    qkv_near = run(project, normed, normed_far, w_qkv, tables)
    att_near = run(attend, qkv_near)
    w_up_far = from_all(chain.wait(piece_up))
    piece_down, cot_low, cot_high = chain(
        lambda w, c: (dp_piece(w), c[:half], c[half:]), w_down, cotangent
    )
    piece_down = swap(piece_down, 0, 2)
    cot_high, cot_low = swap(cot_high, 0, 1), swap(cot_low, 0, 1)
    qkv_far = run(project, normed, normed_far, w_qkv_far, tables)
    att_far = run(attend, qkv_far)
    piece_down, cot_high, cot_low = chain.wait(piece_down, cot_high, cot_low)
    w_down_far = from_all(piece_down)
    heads = (att_near, att_far, w_out, w_out_far)
    low, high = chain(lambda *a: head_rows(place, True, *a), *heads)
    high, low = swap(high, 0, 1), swap(low, 0, 1)
    stay_low, stay_high = chain(lambda *a: head_rows(place, False, *a), *heads)
    norm_args = (gain_two, shift_two)
    normed_high, resid_high = chain(
        lambda *a: second_norm(place, 1, *a), stay_high, tokens, high, *norm_args
    )
    normed_high_far = swap(normed_high, 0, 1)
    normed_low, resid_low = chain(
        lambda *a: second_norm(place, 0, *a), stay_low, tokens, low, *norm_args
    )
    normed_low_far = swap(normed_low, 0, 1)

    weights = (w_up, w_down, w_up_far, w_down_far)
    *kept, stay_high, leave_high = chain(
        lambda *a: feed(0, place, *a), normed_high, normed_high_far, cotangent, cot_high, weights
    )
    back_high = swap(leave_high, 0, 1)
    *kept, stay_low, leave_low = chain(
        lambda *a: feed(1, place, *a), normed_low, normed_low_far, cotangent, cot_low, weights, kept
    )
    back_low = swap(leave_low, 0, 1)
    hidden_near, pre_near, hidden_far, pre_far, rows_two, grad_rows = kept
    ups = ((rows_two, rows_two), (pre_near, pre_far))
    downs = ((hidden_near, hidden_far), (grad_rows, grad_rows))
    grad_high, wide_high, gain_high, shift_high = chain(
        lambda *a: second_back(place, 1, *a), resid_high, stay_high, back_high, cotangent, gain_two
    )
    up = chain(lambda *a: wide_grad(place, None, *a), *ups)
    grad_low, wide_low, gain_low, shift_low = chain(
        lambda *a: second_back(place, 0, *a), resid_low, stay_low, back_low, cotangent, gain_two
    )
    grad_high_far, grad_low_far = swap(grad_high, 0, 1), swap(grad_low, 0, 1)
    down = chain(lambda *a: wide_grad(place, None, *a), *downs)
    out_high_leave, out_low_leave, out_high, out_low = run(
        down_rows, hidden_near, hidden_far, w_down, w_down_far, resid_high, resid_low
    )
    grad_high_far, grad_low_far = chain.wait(grad_high_far, grad_low_far)

    up, down = swap(up, 1, 0), swap(down, 1, 0)
    own, other = (grad_low, grad_high), (grad_low_far, grad_high_far)
    proj_far = chain(
        lambda *a: attend_back(place, LONG, *a), qkv_far, own, other, w_out_far, tables
    )
    up, down = chain.wait(up, down)
    up_keep, up = chain(lambda *a: wide_grad(place, 1, *a), *ups, up)
    down_keep, down = chain(lambda *a: wide_grad(place, 2, *a), *downs, down)
    up, down = swap(up, 2, 0), swap(down, 4, 0)
    proj_near = chain(lambda *a: attend_back(place, 1, *a), qkv_near, own, other, w_out, tables)
    leave_one = chain(
        lambda *a: back_rows(place, True, *a), proj_near, proj_far, w_qkv, w_qkv_far
    )
    attended = (att_near[None], att_far[None])
    kept = chain(
        lambda *a: narrow_grad(place, None, 0, 4, *a), normed, normed_far, proj_near, proj_far
    )
    kept = chain(
        lambda *a: narrow_grad(place, None, 3, 4, *a[:4], kept=a[4]), own, other, *attended, kept
    )
    up, down = chain.wait(up, down)
    up_keep, up = chain(lambda *a: add_split(place, 2, *a), up_keep, up)
    down_keep, down = chain(lambda *a: add_split(place, 1, *a), down_keep, down)
    up, down = swap(up, 4, 0), swap(down, 2, 0)
    heads_grad, back_one = swap(kept[0], 1, 0), swap(leave_one, 0, 1)
    stay_one = chain(
        lambda *a: back_rows(place, False, *a), proj_near, proj_far, w_qkv, w_qkv_far
    )
    heads_grad = chain.wait(heads_grad)
    kept = chain(
        lambda *a: narrow_grad(place, 1, 0, 4, *a),
        normed,
        normed_far,
        proj_near,
        proj_far,
        heads_grad,
    )
    heads_keep, heads_grad = chain(
        lambda *a: narrow_grad(place, 1, 3, 4, *a[:5], kept=a[5]),
        own,
        other,
        *attended,
        heads_grad,
        kept,
    )
    heads_grad = swap(heads_grad, 2, 0)
    up, down, back_one = chain.wait(up, down, back_one)

    def last_step(keep, arrived, hops):
        near, far = run(add_last, keep, arrived)
        return near, swap(far, 0, hops)

    def gather(near, arrived):
        piece = run(add_pair, near, arrived)
        for bit in range(3, bits):
            size = piece.shape[1] // 2
            side = (dp_at >> bit) & 1
            mine = lax.dynamic_slice_in_dim(piece, side * size, size, 1)
            theirs = lax.dynamic_slice_in_dim(piece, (1 - side) * size, size, 1)
            piece = add_pair(place, mine, swap(theirs, 1 << bit, 0))
        return lax.all_gather(piece, "dp", axis=0, tiled=False)

    def order_table(order):
        order = order + list(range(3, bits))
        return jnp.asarray(
            [
                sum(((j >> (bits - 1 - i)) & 1) << bit for i, bit in enumerate(order))
                for j in range(dp_size)
            ],
            jnp.int32,
        )

    up_near, up_far = last_step(up_keep, up, 2)
    down_near, down_far = last_step(down_keep, down, 2)
    out_high_far, out_low_far = swap(out_high_leave, 0, 1), swap(out_low_leave, 0, 1)
    grad_tokens, gain_sum, shift_sum = run(
        first_back, tokens, stay_one, back_one, wide_low, wide_high, gain_one
    )
    sums = chain(
        lambda *a: jnp.concatenate(a, axis=0),
        gain_sum,
        shift_sum,
        gain_low + gain_high,
        shift_low + shift_high,
    )
    steps = [(1 << b, 0) for b in range(bits)] + [(0, 1), (0, 2)]

    def sum_step(sums):
        return chain(lambda a, b: a + b, sums, swap(sums, *steps.pop()))

    heads_keep, heads_grad = chain(lambda *a: add_split(place, 2, *a), heads_keep, heads_grad)
    heads_grad = swap(heads_grad, 4, 0)
    sums = sum_step(sums)
    up_all = gather(up_near, up_far)
    sums = sum_step(sums)
    heads_near, heads_far = last_step(heads_keep, heads_grad, 2)
    down_all = gather(down_near, down_far)
    sums = sum_step(sums)
    heads_all = gather(heads_near, heads_far)
    while steps:
        sums = sum_step(sums)
    layer_out = run(layer_rows, out_low, out_high, out_low_far, out_high_far)

    xy, yx = order_table([0, 1, 2]), order_table([0, 2, 1])
    grad_up = chain(lambda v: assemble(xy, v), up_all)[0]
    grad_down = chain(lambda v: assemble(yx, v), down_all)[0]
    grad_qkv, grad_out = chain(lambda v: assemble_heads(xy, v), heads_all)
    return (
        layer_out,
        grad_tokens,
        sums[0],
        sums[1],
        grad_qkv,
        grad_out,
        sums[2],
        sums[3],
        grad_up,
        grad_down,
    )


def solution(mesh):
    rows = P(AXES, None)
    params = (P(), P(), P(None, None, "tensor"), P("tensor", None))
    wide = (P(None, "tensor"), P("tensor", None))
    return jax.shard_map(
        shards,
        mesh=mesh,
        in_specs=(rows, P("dp")) + params + (P(), P()) + wide + (rows,),
        out_specs=(rows, rows) + params + (P(), P()) + wide,
        check_vma=False,
    )
```

```python
import functools
import math

import jax
import jax.numpy as jnp
import numpy as np
from jax import lax
from jax.experimental import pallas as pl
from jax.experimental.pallas import tpu as pltpu
from jax.sharding import PartitionSpec as P

HD = 128
FF = 6144
EPS = 1e-05
AXES = ("dp", "tensor")
BF = jnp.bfloat16
F32 = jnp.float32
LOG2E = 1.4426950408889634
LONG = 200_000_000_000
VMEM_LIMIT = 56 * 1024 * 1024
VMEM_SPARE = 10 * 1024 * 1024

ODD, SIDE, LIMIT, NEAR_UNIT, FAR_UNIT = 0, 1, 4, 5, 6

NN = (((1,), (0,)), ((), ()))
NT = (((1,), (1,)), ((), ()))
TN = (((0,), (0,)), ((), ()))


def mm(a, b, dims=NN):
    return lax.dot_general(a, b, dims, preferred_element_type=F32)


def swap(value, dp_bits, tensor_bits):
    dp_size = lax.axis_size("dp")
    tensor_size = lax.axis_size("tensor")
    pairs = [
        (d * tensor_size + t, (d ^ dp_bits) * tensor_size + (t ^ tensor_bits))
        for d in range(dp_size)
        for t in range(tensor_size)
    ]
    return lax.ppermute(value, AXES, pairs)


class Chain:
    def __init__(self):
        self.last = None

    def __call__(self, call, *args):
        if self.last is not None:
            leaves, tree = jax.tree.flatten(args)
            leaves = lax.optimization_barrier(tuple(leaves) + (self.last,))[:-1]
            args = jax.tree.unflatten(tree, leaves)
        out = call(*args)
        self.last = jax.tree.leaves(out)[0]
        return out

    def wait(self, *args):
        return self(lambda *v: v[0] if len(v) == 1 else v, *args)


def dp_piece(weight):
    rows = weight.shape[0] // lax.axis_size("dp")
    return lax.dynamic_slice_in_dim(weight, lax.axis_index("dp") * rows, rows, 0)


def from_all(piece):
    return lax.all_gather(piece, "dp", axis=0, tiled=True)


def stacked_from_all(piece):
    whole = lax.all_gather(piece, "dp", axis=0, tiled=False)
    if piece.shape[1] % 16 == 0:
        return whole
    return whole.transpose(1, 0, 2, 3).reshape(1, 2, -1, piece.shape[2])


def block(shape, index=None):
    if index is None:
        return pl.BlockSpec(shape, lambda *_: (0,) * len(shape))
    return pl.BlockSpec(shape, index)


def shape_of(shape, kind=BF):
    return jax.ShapeDtypeStruct(shape, kind)


def kernel(body, grid, ins, outs, shapes, scratch=(), aliases=None, cost=1):
    def call(place, *args):
        pairs = list(zip(ins, args)) + list(zip(jax.tree.leaves(outs), jax.tree.leaves(shapes)))
        blocks = [
            2 * math.prod(spec.block_shape) * array.dtype.itemsize
            for spec, array in pairs
            if spec.block_shape is not None
        ]
        blocks += [math.prod(one.shape) * jnp.dtype(one.dtype).itemsize for one in scratch]
        return pl.pallas_call(
            body,
            grid_spec=pltpu.PrefetchScalarGridSpec(
                num_scalar_prefetch=1,
                grid=grid,
                in_specs=ins,
                out_specs=outs,
                scratch_shapes=list(scratch),
            ),
            out_shape=shapes,
            input_output_aliases=aliases or {},
            compiler_params=pltpu.CompilerParams(
                vmem_limit_bytes=min(VMEM_LIMIT, sum(blocks) + VMEM_SPARE)
            ),
            cost_estimate=pl.CostEstimate(flops=cost, bytes_accessed=1, transcendentals=0),
        )(place, *args)

    return call


def rows_at(start, size):
    return pl.ds(pl.multiple_of(start, size), size)


def norm_stats(values):
    center = values - jnp.mean(values, axis=-1, keepdims=True)
    spread = jnp.mean(center * center, axis=-1, keepdims=True)
    inverse = lax.rsqrt(spread + EPS)
    return center * inverse, inverse


def norm_back(grads, normal, inverse, gain):
    scaled = grads * gain
    mean_one = jnp.mean(scaled, axis=-1, keepdims=True)
    mean_two = jnp.mean(scaled * normal, axis=-1, keepdims=True)
    return (
        inverse * (scaled - mean_one - normal * mean_two),
        jnp.sum(grads * normal, axis=0, keepdims=True),
        jnp.sum(grads, axis=0, keepdims=True),
    )


def first_norm(place, tokens, gain, shift):
    rows, depth = tokens.shape
    half = rows // 2

    def body(_, x, gain, shift, low, high):
        normal, _ = norm_stats(x[...].astype(F32))
        value = (normal * gain[...] + shift[...]).astype(BF)
        pl.when(pl.program_id(0) == 0)(lambda: low.__setitem__(..., value))
        pl.when(pl.program_id(0) == 1)(lambda: high.__setitem__(..., value))

    return kernel(
        body,
        (2,),
        [block((half, depth), lambda i, _: (i, 0))] + [block((1, depth))] * 2,
        [block((half, depth))] * 2,
        [shape_of((half, depth))] * 2,
    )(place, tokens, gain, shift)


def rope_tables(length):
    frequency = np.exp(
        np.arange(HD // 2, dtype=np.float32) * np.float32(-2.0 * math.log(10000.0) / HD)
    ).astype(np.float32)
    angles = (np.arange(length, dtype=np.float32)[:, None] * frequency[None, :]).astype(np.float64)
    cos_part, sin_part = np.cos(angles), np.sin(angles)
    return (
        np.concatenate([cos_part, cos_part], axis=1).astype(np.float32),
        np.concatenate([-sin_part, sin_part], axis=1).astype(np.float32),
    )


def project(place, own, other, weight, tables, through=None):
    part, depth = own[0].shape
    width = weight.shape[2]

    def body(p, ol, oh, tl, th, weight, cos, sin, *refs):
        out = refs[-1]
        if through is not None:
            out = refs[1]
            pl.when(pl.program_id(0) < 2)(lambda: refs[2].__setitem__(..., refs[0][...]))
            pl.when(pl.program_id(0) >= 2)(lambda: refs[3].__setitem__(..., refs[0][...]))

        def go(source):
            x = source[...]
            for c in range(3):
                result = mm(x, weight[c])
                if c == 2:
                    out[c] = result.astype(BF)
                    continue
                for h in range(width // HD):
                    one = result[:, h * HD : (h + 1) * HD]
                    turned = one * cos[...] + pltpu.roll(one, HD // 2, 1) * sin[...]
                    out[c, :, h * HD : (h + 1) * HD] = turned.astype(BF)

        step = pl.program_id(0)
        at = jnp.where(step // 2 == p[ODD], 0, 2) + step % 2
        for i, source in enumerate((ol, oh, tl, th)):
            pl.when(at == i)(functools.partial(go, source))

    table = block((part, HD), lambda i, _: (i, 0))
    size = part // 2
    ins, outs = [], []
    if through is not None:
        ins = [block((size, depth), lambda i, _: (i, 0))]
        outs = [
            block((size, depth), lambda i, _: (jnp.minimum(i, 1), 0)),
            block((size, depth), lambda i, _: (jnp.maximum(i - 2, 0), 0)),
        ]
    return kernel(
        body,
        (4,),
        [block((part, depth))] * 4 + [block((3, depth, width)), table, table] + ins,
        [block((3, part, width), lambda i, _: (0, i, 0))] + outs,
        [shape_of((3, 4 * part, width))] + [shape_of((part, depth))] * len(outs),
    )(place, *own, *other, weight, *tables, *([through] if ins else []))


QB = 256


EXP_SCALE = HD ** (-0.5) * LOG2E


def masked(scores):
    key_at = lax.broadcasted_iota(jnp.int32, scores.shape, 0)
    row_at = lax.broadcasted_iota(jnp.int32, scores.shape, 1)
    return jnp.where(key_at <= row_at, scores, -1e30)


def probs_t(q, k_ref, first):
    diagonal = masked(mm(k_ref[0, first : first + QB], q, NT))
    top = jnp.max(diagonal, axis=0, keepdims=True)
    before = None
    if first:
        before = mm(k_ref[0, :first], q, NT)
        top = jnp.maximum(top, jnp.max(before, axis=0, keepdims=True))
    diagonal = jnp.exp2((diagonal - top) * EXP_SCALE)
    total = jnp.sum(diagonal, axis=0, keepdims=True)
    if first:
        before = jnp.exp2((before - top) * EXP_SCALE)
        total = total + jnp.sum(before, axis=0, keepdims=True)
    return before, diagonal, 1.0 / total


def attend(place, far, qkv, kept=()):
    _, length, width = qkv.shape
    heads = width // HD

    def body(_, q_ref, k_ref, v_ref, *refs):
        out_ref = refs[-1]
        for first in range(0, length, QB):
            last = first + QB
            before, diagonal, inverse = probs_t(q_ref[0, first:last], k_ref, first)
            blended = mm(v_ref[0, first:last], diagonal.astype(BF), TN)
            if first:
                blended = blended + mm(v_ref[0, :first], before.astype(BF), TN)
            out_ref[first:last, :] = (blended * inverse).T.astype(BF)

    spec = lambda c: block((1, length, HD), lambda h, _: (c, 0, h))
    return kernel(
        body,
        (heads,),
        [spec(0), spec(1), spec(2)] + [pl.BlockSpec(memory_space=pl.ANY)] * len(kept),
        [block((length, HD), lambda h, _: (0, h + heads * far))],
        [shape_of((length, 2 * width))],
        aliases={4 + i: i for i in range(len(kept))},
    )(place, qkv, qkv, qkv, *kept)


def attend_back(place, far, cost, qkv, own, other, w_out, tables, kept=()):
    _, length, width = qkv.shape
    heads = width // HD
    depth = w_out.shape[1]
    part = length // 4

    def unturn(grads, cos, sin):
        return (grads * cos - pltpu.roll(grads, HD // 2, 1) * sin).astype(BF)

    def body(p, q_ref, k_ref, v_ref, ol, oh, tl, th, w_ref, cos, sin, *refs):
        out, g_ref, dk_ref, dv_ref = refs[-4:]
        for base, low, high in ((p[ODD] * 2, ol, oh), ((1 - p[ODD]) * 2, tl, th)):
            g_ref[rows_at(base * part, part)] = mm(low[...], w_ref[...], NT).astype(BF)
            g_ref[rows_at((base + 1) * part, part)] = mm(high[...], w_ref[...], NT).astype(BF)
        for first in reversed(range(0, length, QB)):
            last = first + QB
            q = q_ref[0, first:last]
            g = g_ref[first:last]
            *weights, inverse = probs_t(q, k_ref, first)
            parts = []
            inner = 0.0
            for weight, here in zip(weights, (slice(0, first), slice(first, last))):
                if weight is None:
                    continue
                grad_probs = mm(v_ref[0, here], g, NT)
                inner = inner + jnp.sum(weight * grad_probs, axis=0, keepdims=True)
                parts.append((here, weight, grad_probs))
            inner = inner * inverse
            scaled = inverse * HD ** (-0.5)
            grad_q = 0.0
            for here, weight, grad_probs in parts:
                grad_scores = (weight * ((grad_probs - inner) * scaled)).astype(BF)
                grad_v = mm((weight * inverse).astype(BF), g)
                grad_k = mm(grad_scores, q)
                if last == length:
                    dv_ref[here] = grad_v
                    dk_ref[here] = grad_k
                else:
                    dv_ref[here] += grad_v
                    dk_ref[here] += grad_k
                grad_q = grad_q + mm(grad_scores, k_ref[0, here], TN)
            out[0, first:last] = unturn(grad_q, cos[first:last], sin[first:last])
        out[1] = unturn(dk_ref[...], cos[...], sin[...])
        out[2] = dv_ref[...].astype(BF)

    spec = lambda c: block((1, length, HD), lambda h, _: (c, 0, h))
    piece = block((part, depth))
    table = block((length, HD))
    return kernel(
        body,
        (heads,),
        [spec(0), spec(1), spec(2)]
        + [piece] * 4
        + [block((HD, depth), lambda h, _: (h, 0)), table, table]
        + [pl.BlockSpec(memory_space=pl.ANY)] * len(kept),
        [block((3, length, HD), lambda h, _: (0, 0, h + heads * far))],
        [shape_of((3, length, 2 * width))],
        [pltpu.VMEM((length, HD), BF), pltpu.VMEM((length, HD), F32), pltpu.VMEM((length, HD), F32)],
        {11 + i: i for i in range(len(kept))},
        cost,
    )(place, qkv, qkv, qkv, *own, *other, w_out, *tables, *kept)


def head_rows(place, leave, heads, w_near, w_far):
    length, width = heads.shape
    depth = w_near.shape[1]
    half = length // 4
    kind = BF if leave else F32
    cols = depth // 2

    def body(_, heads, w_near, w_far, low, high):
        total = mm(heads[...], jnp.concatenate([w_near[...], w_far[...]], axis=0))
        low[...] = total[:half].astype(kind)
        high[...] = total[half:].astype(kind)

    weight = block((width // 2, cols), lambda i, p: (0, i))
    return kernel(
        body,
        (2,),
        [
            block((2 * half, width), lambda i, p: (1 - p[ODD] if leave else p[ODD], 0)),
            weight,
            weight,
        ],
        [block((half, cols), lambda i, p: (0, i))] * 2,
        [shape_of((half, depth), kind)] * 2,
    )(place, heads, w_near, w_far)


def second_norm(place, which, stay, tokens, arrived, gain, shift):
    half, depth = stay.shape
    size = half // 2

    def body(_, stay, tokens, arrived, gain, shift, normed, resid):
        total = tokens[...].astype(F32) + stay[...] + arrived[...].astype(F32)
        resid[...] = total
        normal, _ = norm_stats(total)
        normed[...] = (normal * gain[...] + shift[...]).astype(BF)

    piece = block((size, depth), lambda i, _: (i, 0))
    return kernel(
        body,
        (2,),
        [piece, block((size, depth), lambda i, _: (2 * which + i, 0)), piece]
        + [block((1, depth))] * 2,
        [piece] * 2,
        [shape_of((half, depth)), shape_of((half, depth), F32)],
    )(place, stay, tokens, arrived, gain, shift)


def gelu_pair(v):
    c = math.sqrt(2.0 / math.pi)
    square = v * v
    t = jnp.tanh(v * (c + (c * 0.044715) * square))
    half = 0.5 + 0.5 * t
    slope = half + v * (0.5 - 0.5 * t * t) * (c + (3.0 * 0.044715 * c) * square)
    return v * half, slope


UB = 768
SB = 256


def hidden_grads(place, cost, rows_in, weight):
    each, depth = rows_in[0].shape
    count = each * len(rows_in)
    parts, _, rows, _ = weight.shape
    units = parts * rows
    step = UB // rows if rows < UB else 1
    tile = (step, 1, min(rows, UB), depth)
    last = weight.shape[1] - 1

    def body(_, *refs):
        *sources, weight, out = refs
        w = weight[:, 0].reshape(UB, depth)
        for i, source in enumerate(sources):
            out[i * each : (i + 1) * each] = mm(source[...], w, NT).astype(BF)

    place_of = lambda j: (j, last, 0, 0) if rows <= UB else (0, last, j, 0)
    return kernel(
        body,
        (units // UB,),
        [block((each, depth))] * len(rows_in) + [block(tile, lambda j, _: place_of(j))],
        block((count, UB), lambda j, _: (0, j)),
        shape_of((count, units)),
        cost=cost,
    )(place, *rows_in, weight)


def feed(group, place, normed, normed_far, cot, cot_far, w_up, far_pair, hidden_grad, kept=()):
    half, depth = normed.shape
    size = 2 * half
    units = w_up.shape[1]
    near_steps = units // UB
    far_parts, _, far_rows, _ = far_pair.shape

    def body(p, own, other, g_own, g_other, un, uf, gno, gnt, gfo, gft, *refs):
        hn, pn, hf, pf, rows, grads, stay, leave, total = refs[-9:]
        step = pl.program_id(0)

        @pl.when(step == 0)
        def _():
            total[...] = jnp.zeros_like(total)
            rows[:half] = own[...]
            rows[half:] = other[...]
            grads[:half] = g_own[...]
            grads[half:] = g_other[...]

        def work(up, grad_own, grad_other, hidden, pre):
            for at in range(0, UB, SB):
                there = slice(at, at + SB)
                value, slope = gelu_pair(mm(rows[...], up[:, there]))
                hidden[:, there] = value.astype(BF)
                pre[:half, there] = (grad_own[:, there].astype(F32) * slope[:half]).astype(BF)
                pre[half:, there] = (grad_other[:, there].astype(F32) * slope[half:]).astype(BF)
            total[...] += mm(pre[...], up, NT)

        def part(first_unit, up, grad_own, grad_other, hidden, pre):
            live = first_unit < p[LIMIT]

            @pl.when(live)
            def _():
                work(up(), grad_own, grad_other, hidden, pre)

            @pl.when(jnp.logical_not(live))
            def _():
                hidden[...] = jnp.zeros((size, UB), BF)
                pre[...] = jnp.zeros((size, UB), BF)

        @pl.when(step < near_steps)
        def _():
            part(p[NEAR_UNIT] + step * UB, lambda: un[...], gno, gnt, hn, pn)

        @pl.when(step >= near_steps)
        def _():
            far_up = lambda: uf[:, 0].reshape(depth, UB)
            part(p[FAR_UNIT] + (step - near_steps) * UB, far_up, gfo, gft, hf, pf)

        @pl.when(step == 2 * near_steps - 1)
        def _():
            stay[...] = total[:half]
            leave[...] = total[half:].astype(BF)

    near = lambda j: jnp.minimum(j, near_steps - 1)
    far = lambda j: jnp.maximum(j - near_steps, 0)
    wide = [block((size, UB), lambda j, _, at=at: (group, at(j))) for at in (near, far)]
    slim = [block((half, UB), lambda j, _, at=at: (1 - group, at(j))) for at in (near, far)]
    piece = block((half, depth))
    rows = block((size, depth), lambda j, _: (group, 0))
    return kernel(
        body,
        (2 * near_steps,),
        [piece, piece, block((half, depth), lambda j, _: (1 - group, 0)), piece]
        + [block((depth, UB), lambda j, _: (0, near(j)))]
        + [block((far_parts, 1, far_rows, UB), lambda j, _: (0, 0, 0, far(j)))]
        + [slim[0], slim[0], slim[1], slim[1]]
        + [pl.BlockSpec(memory_space=pl.ANY)] * len(kept),
        [wide[0], wide[0], wide[1], wide[1], rows, rows, piece, piece],
        [shape_of((2 * size, units))] * 4
        + [shape_of((2 * size, depth))] * 2
        + [shape_of((half, depth), F32), shape_of((half, depth))],
        [pltpu.VMEM((size, depth), F32)],
        {11 + i: i for i in range(len(kept))},
    )(place, normed, normed_far, cot, cot_far, w_up, far_pair, *hidden_grad, *kept)


def second_back(place, which, resid, stay, arrived, cot, gain):
    half, depth = resid.shape
    size = half // 2

    def body(_, resid, stay, arrived, cot, gain, low, wide, gain_sum, shift_sum):
        normal, inverse = norm_stats(resid[...])
        grad, gains, shifts = norm_back(
            stay[...] + arrived[...].astype(F32), normal, inverse, gain[...]
        )
        grad = grad + cot[...].astype(F32)
        wide[...] = grad
        low[...] = grad.astype(BF)

        @pl.when(pl.program_id(0) == 0)
        def _():
            gain_sum[...] = gains
            shift_sum[...] = shifts

        @pl.when(pl.program_id(0) > 0)
        def _():
            gain_sum[...] += gains
            shift_sum[...] += shifts

    piece = block((size, depth), lambda i, _: (i, 0))
    vector = block((1, depth))
    return kernel(
        body,
        (2,),
        [piece] * 3 + [block((size, depth), lambda i, _: (2 * which + i, 0)), vector],
        [piece, piece, vector, vector],
        [shape_of((half, depth)), shape_of((half, depth), F32)] + [shape_of((1, depth), F32)] * 2,
    )(place, resid, stay, arrived, cot, gain)


def down_rows(place, near, far, w_near, far_pair, resid_high, resid_low):
    rows, units = near.shape
    depth = w_near.shape[1]
    half = rows // 4
    cols = depth // 3
    far_parts, _, far_rows, _ = far_pair.shape

    def body(_, near, far, w_near, w_far, resid_high, resid_low, high, low, out_high, out_low):
        w_second = w_far[:, 0].reshape(units, cols)
        for i, (stay, resid, leave) in enumerate(
            ((out_high, resid_high, high), (out_low, resid_low, low))
        ):
            here = slice(2 * i * half, 2 * (i + 1) * half)
            total = mm(near[here], w_near[...]) + mm(far[here], w_second)
            stay[...] = total[:half] + resid[...]
            leave[...] = total[half:].astype(BF)

    hidden = block((rows, units))
    piece = block((half, cols), lambda j, _: (0, j))
    return kernel(
        body,
        (3,),
        [
            hidden,
            hidden,
            block((units, cols), lambda j, _: (0, j)),
            block((far_parts, 1, far_rows, cols), lambda j, _: (0, 1, 0, j)),
            piece,
            piece,
        ],
        [piece] * 4,
        [shape_of((half, depth))] * 2 + [shape_of((half, depth), F32)] * 2,
        cost=LONG,
    )(place, near, far, w_near, far_pair, resid_high, resid_low)


def layer_rows(place, out_low, out_high, low, high):
    half, depth = low.shape

    def body(_, out_low, out_high, low, high, out):
        out[:half] = (out_low[...] + low[...].astype(F32)).astype(BF)
        out[half:] = (out_high[...] + high[...].astype(F32)).astype(BF)

    piece = block((half, depth))
    return kernel(body, (1,), [piece] * 4, block((2 * half, depth)), shape_of((2 * half, depth)))(
        place, out_low, out_high, low, high
    )


def wide_grad(place, bit, lefts, rights, arrived=None):
    rows, width = lefts[0].shape
    depth = rights[0].shape[1]
    half = width // 2
    cols = depth // 2
    last = arrived is not None

    def body(p, l0, l1, r0, r1, *refs):
        turned = refs[-1]
        shard = pl.program_id(0)

        @pl.when(pl.program_id(1) == 0)
        def _():
            pl.when(shard == 0)(lambda: turned.__setitem__(..., l0[...].T))
            pl.when(shard == 1)(lambda: turned.__setitem__(..., l1[...].T))

        def go(right):
            if not last:
                refs[0][0, 0] = mm(turned[...], right[...]).astype(BF)
                return
            for out, side in ((refs[1], p[SIDE + bit]), (refs[2], 1 - p[SIDE + bit])):
                here = rows_at(side * (half // 2), half // 2)
                value = mm(turned[here], right[...]) + refs[0][0, 0, here].astype(F32)
                out[0, 0] = value.astype(BF)

        pl.when(shard == 0)(lambda: go(r0))
        pl.when(shard == 1)(lambda: go(r1))

    side = lambda p: p[SIDE] if last else 1 - p[SIDE]
    left = block((rows, half), lambda s, j, p: (0, side(p)))
    right = lambda shard: block(
        (rows, cols), lambda s, j, p: (0, jnp.where(s == shard, j, 1 - shard))
    )
    tall = lambda size: block((1, 1, size, cols), lambda s, j, p: (s, 0, 0, j))
    if last:
        outs = [tall(half // 2)] * 2
        shapes = [shape_of((2, 1, half // 2, depth))] * 2
    else:
        outs, shapes = tall(half), shape_of((2, 1, half, depth))
    return kernel(
        body,
        (2, 2),
        [left, left, right(0), right(1)] + [tall(half)] * last,
        outs,
        shapes,
        [pltpu.VMEM((half, rows), BF)],
    )(place, *lefts, *rights, *([arrived] if last else []))


def narrow_grad(place, own, other, rights, dests, arrived=(), kept=()):
    rows, depth = own[0].shape
    parts = len(own)
    count, length, width = rights.shape
    half = depth // 2
    last = len(arrived) > 0
    n_out = 2 if last else 1
    size = half // 2 if last else half

    def body(p, *refs):
        own, other, right = refs[:parts], refs[parts : 2 * parts], refs[2 * parts]
        got = refs[2 * parts + 1 : 2 * parts + 1 + len(arrived)]
        outs, turned = refs[-1 - n_out * len(dests) : -1], refs[-1]
        c = pl.program_id(0)

        @pl.when(c == 0)
        def _():
            for lefts, base in ((own, p[ODD]), (other, 1 - p[ODD])):
                for i, left in enumerate(lefts):
                    turned[:, rows_at((base * parts + i) * rows, rows)] = left[...].T

        def go(i, bit):
            if not last:
                value = mm(turned[...], right[0]).astype(BF)
                outs[i][0, 0] = value[:, : width // 2]
                outs[i][1, 0] = value[:, width // 2 :]
                return
            for out, side in ((outs[2 * i], p[SIDE + bit]), (outs[2 * i + 1], 1 - p[SIDE + bit])):
                here = rows_at(side * size, size)
                value = mm(turned[here], right[0])
                for shard in range(2):
                    there = slice(shard * width // 2, (shard + 1) * width // 2)
                    out[shard, 0] = (value[:, there] + got[i][shard, 0, here].astype(F32)).astype(BF)

        for i, (first, many, _, _, bit) in enumerate(dests):
            pl.when((c >= first) & (c < first + many))(functools.partial(go, i, bit))

    side = lambda p: p[SIDE] if last else 1 - p[SIDE]
    left = block((rows, half), lambda c, p: (0, side(p)))

    def tall(dest, size):
        first, many, _, at, _ = dest
        return block(
            (2, 1, size, width // 2), lambda c, p: (0, at + jnp.clip(c - first, 0, many - 1), 0, 0)
        )

    ins = [left] * (2 * parts) + [block((1, length, width), lambda c, p: (c, 0, 0))]
    ins += [tall(dest, half) for dest in dests] * last
    return kernel(
        body,
        (count,),
        ins + [pl.BlockSpec(memory_space=pl.ANY)] * len(kept),
        [tall(dest, size) for dest in dests for _ in range(n_out)],
        [shape_of((2, dest[2], size, width // 2)) for dest in dests for _ in range(n_out)],
        [pltpu.VMEM((half, length), BF)],
        {1 + len(ins) + i: i for i in range(len(kept))},
    )(place, *own, *other, rights, *arrived, *kept)


def add_split(place, bits, *pairs):
    _, count, rows, width = pairs[0].shape
    half = rows // 2

    def body(p, *refs):
        for i, bit in enumerate(bits):
            mine, theirs = refs[2 * i : 2 * i + 2]
            outs = refs[2 * (len(bits) + i) : 2 * (len(bits) + i) + 2]
            for out, side in zip(outs, (p[SIDE + bit], 1 - p[SIDE + bit])):
                here = rows_at(side * half, half)
                out[0, 0] = (mine[0, 0, here].astype(F32) + theirs[0, 0, here].astype(F32)).astype(BF)

    full = block((1, 1, rows, width), lambda s, c, p: (s, c, 0, 0))
    out = block((1, 1, half, width), lambda s, c, p: (s, c, 0, 0))
    n = 2 * len(bits)
    return kernel(
        body, (2, count), [full] * n, [out] * n, [shape_of((2, count, half, width))] * n
    )(place, *pairs)


def add_last(place, *pairs):
    _, count, rows, width = pairs[0].shape
    n = len(pairs) // 2

    def body(_, *refs):
        near, far = refs[-2:]
        for i in range(n):
            for shard, out in ((0, near), (1, far)):
                for c in range(count):
                    mine, theirs = refs[2 * i][shard, c], refs[2 * i + 1][shard, c]
                    out[i * count + c] = (mine.astype(F32) + theirs.astype(F32)).astype(BF)

    full = block((2, count, rows, width))
    out = block((n * count, rows, width))
    return kernel(
        body, (1,), [full] * (2 * n), [out, out], [shape_of((n * count, rows, width))] * 2
    )(place, *pairs)


def add_pair(place, near, arrived):
    shape = near.shape

    def body(_, mine, theirs, out):
        out[...] = (mine[...].astype(F32) + theirs[...].astype(F32)).astype(BF)

    full = block(shape)
    return kernel(body, (1,), [full, full], full, shape_of(shape))(place, near, arrived)


def assemble(table, whole):
    size, _, rows, width = whole.shape

    def body(_, one, two, out_one, out_two):
        out_one[...] = one[0, 0].astype(F32)
        out_two[...] = two[0, 0].astype(F32)

    piece = lambda i: block((1, 1, rows, width), lambda j, t: (t[size * i + j], i, 0, 0))
    return kernel(
        body,
        (size,),
        [piece(0), piece(1)],
        [block((rows, width), lambda j, t: (j, 0))] * 2,
        [shape_of((rows * size, width), F32)] * 2,
    )(table, whole, whole)


def assemble_heads(table, whole):
    size, count, rows, width = whole.shape
    group = 2 if 2 * rows % 128 == 0 else size

    def body(_, *refs):
        pieces, (out, last) = refs[:-2], refs[-2:]
        for i in range(group):
            here = slice(i * rows, (i + 1) * rows)
            one, two = pieces[2 * i : 2 * i + 2]
            out[:2, here] = one[0].astype(F32)
            out[2, here] = two[0, 0].astype(F32)
        turned = jnp.concatenate([pieces[2 * i + 1][0, 1] for i in range(group)], axis=0)
        last[...] = turned.astype(F32).T

    piece = lambda i, k: block(
        (1, 2, rows, width), lambda j, t: (t[size * k + group * j + i], k, 0, 0)
    )
    return kernel(
        body,
        (size // group,),
        [piece(i, k) for i in range(group) for k in range(2)],
        [
            block((count - 1, group * rows, width), lambda j, t: (0, j, 0)),
            block((width, group * rows), lambda j, t: (0, j)),
        ],
        [shape_of((count - 1, rows * size, width), F32), shape_of((width, rows * size), F32)],
    )(table, *([whole] * (2 * group)))


def back_rows(place, leave, proj, w_near, w_far):
    count, length, width = proj.shape
    depth = w_near.shape[1]
    rows = length // 2
    cols = depth // 3
    kind = BF if leave else F32

    def body(_, proj, w_near, w_far, out):
        total = 0.0
        for c in range(count):
            weight = jnp.concatenate([w_near[c], w_far[c]], axis=1)
            total = total + mm(proj[c], weight, NT)
        out[...] = total.astype(kind)

    weight = block((count, cols, width // 2), lambda j, p: (0, j, 0))
    return kernel(
        body,
        (3,),
        [
            block((count, rows, width), lambda j, p: (0, 1 - p[ODD] if leave else p[ODD], 0)),
            weight,
            weight,
        ],
        block((rows, cols), lambda j, p: (0, j)),
        shape_of((rows, depth), kind),
        cost=LONG,
    )(place, proj, w_near, w_far)


def first_back(place, tokens, stay, arrived, resid_low, resid_high, gain):
    rows, depth = tokens.shape
    half = rows // 2

    def body(_, tokens, stay, arrived, resid_low, resid_high, gain, out, gain_sum, shift_sum):
        normal, inverse = norm_stats(tokens[...].astype(F32))
        grad, gains, shifts = norm_back(
            stay[...] + arrived[...].astype(F32), normal, inverse, gain[...]
        )

        @pl.when(pl.program_id(0) == 0)
        def _():
            out[...] = grad + resid_low[...]
            gain_sum[...] = gains
            shift_sum[...] = shifts

        @pl.when(pl.program_id(0) == 1)
        def _():
            out[...] = grad + resid_high[...]
            gain_sum[...] += gains
            shift_sum[...] += shifts

    tile = block((half, depth), lambda i, _: (i, 0))
    piece = block((half, depth))
    vector = block((1, depth))
    return kernel(
        body,
        (2,),
        [tile, tile, tile, piece, piece, vector],
        [tile, vector, vector],
        [shape_of((rows, depth), F32)] + [shape_of((1, depth), F32)] * 2,
        cost=LONG,
    )(place, tokens, stay, arrived, resid_low, resid_high, gain)


def shards(
    tokens,
    granularity,
    gain_one,
    shift_one,
    w_qkv,
    w_out,
    gain_two,
    shift_two,
    w_up,
    w_down,
    cotangent,
):
    tensor_size = lax.axis_size("tensor")
    dp_size = lax.axis_size("dp")
    rank = lax.axis_index("tensor")
    dp_at = lax.axis_index("dp")
    local_rows, depth = tokens.shape
    seq_len = local_rows * tensor_size // granularity.shape[0]
    assert tensor_size == 4 and seq_len == 2 * local_rows and dp_size % 8 == 0
    half = local_rows // 2
    hidden_here = w_up.shape[1]
    head_width = w_qkv.shape[2]
    bits = dp_size.bit_length() - 1
    tables = [jnp.asarray(t) for t in rope_tables(seq_len)]
    gain_one, shift_one, gain_two, shift_two = (
        v[None, :] for v in (gain_one, shift_one, gain_two, shift_two)
    )
    limits = jnp.left_shift(jnp.ones_like(granularity), granularity) * (FF // 8)
    upper = rank // 2
    place = jnp.stack(
        [
            rank % 2,
            dp_at & 1,
            (dp_at >> 1) & 1,
            (dp_at >> 2) & 1,
            jnp.where(upper == 0, limits[0], limits[1]),
            rank * hidden_here,
            (rank ^ 2) * hidden_here,
        ]
    ).astype(jnp.int32)
    chain = Chain()
    run = lambda call, *args: chain(functools.partial(call, place), *args)

    piece_qkv = swap(chain(dp_piece, w_qkv.reshape(3 * depth, head_width)), 0, 2)
    normed = run(first_norm, tokens, gain_one, shift_one)
    normed_far = [swap(v, 0, 1) for v in normed]
    w_down_own = w_down[None, None]
    own_near = chain(lambda *a: hidden_grads(place, LONG, *a), [cotangent], w_down_own)
    normed_far[0], piece_qkv = chain.wait(normed_far[0], piece_qkv)
    w_qkv_far = from_all(piece_qkv).reshape(w_qkv.shape)
    piece_out, piece_pair = chain(
        lambda a, b, c: (dp_piece(a), jnp.stack([dp_piece(b), dp_piece(c)])), w_out, w_up, w_down
    )
    piece_out, piece_pair = swap(piece_out, 0, 2), swap(piece_pair, 0, 2)
    normed_far[1], piece_out = chain.wait(normed_far[1], piece_out)
    w_out_far = from_all(piece_out)
    qkv_near, *cot_far = run(project, normed, normed_far, w_qkv, tables, cotangent)
    cot_far = [swap(v, 0, 1) for v in cot_far]
    heads = chain(lambda *a: attend(place, 0, *a), qkv_near)
    (qkv_far,) = run(project, normed, normed_far, w_qkv_far, tables)
    (heads,) = chain(lambda *a: attend(place, 1, *a), qkv_far, heads)
    cot_far[1], piece_pair = chain.wait(cot_far[1], piece_pair)
    far_pair = stacked_from_all(piece_pair)
    low, high = chain(lambda *a: head_rows(place, True, *a), heads, w_out, w_out_far)
    high, low = swap(high, 0, 1), swap(low, 0, 1)
    stay_low, stay_high = chain(lambda *a: head_rows(place, False, *a), heads, w_out, w_out_far)
    norm_args = (gain_two, shift_two)
    normed_high, resid_high = chain(
        lambda *a: second_norm(place, 1, *a), stay_high, tokens, high, *norm_args
    )
    normed_high_far = swap(normed_high, 0, 1)
    other_near = chain(lambda *a: hidden_grads(place, 1, *a), cot_far, w_down_own)
    normed_low, resid_low = chain(
        lambda *a: second_norm(place, 0, *a), stay_low, tokens, low, *norm_args
    )
    normed_low_far = swap(normed_low, 0, 1)
    other_far = chain(lambda *a: hidden_grads(place, 1, *a), cot_far, far_pair)
    own_far = chain(lambda *a: hidden_grads(place, 1, *a), [cotangent], far_pair)

    weights = (w_up, far_pair, (own_near, other_near, own_far, other_far))
    *kept, stay_high, leave_high = chain(
        lambda *a: feed(0, place, *a), normed_high, normed_high_far, cotangent, cot_far[1], *weights
    )
    back_high = swap(leave_high, 0, 1)
    *kept, stay_low, leave_low = chain(
        lambda *a: feed(1, place, *a),
        normed_low,
        normed_low_far,
        cotangent,
        cot_far[0],
        *weights,
        kept,
    )
    back_low = swap(leave_low, 0, 1)
    hidden_near, pre_near, hidden_far, pre_far, rows_two, grad_rows = kept
    ups = ((rows_two, rows_two), (pre_near, pre_far))
    downs = ((hidden_near, hidden_far), (grad_rows, grad_rows))
    grad_high, wide_high, gain_high, shift_high = chain(
        lambda *a: second_back(place, 1, *a), resid_high, stay_high, back_high, cotangent, gain_two
    )
    up = swap(chain(lambda *a: wide_grad(place, None, *a), *ups), 1, 0)
    down = swap(chain(lambda *a: wide_grad(place, None, *a), *downs), 1, 0)
    up_keep, up = chain(lambda *a: wide_grad(place, 1, *a), *ups, up)
    grad_low, wide_low, gain_low, shift_low = chain(
        lambda *a: second_back(place, 0, *a), resid_low, stay_low, back_low, cotangent, gain_two
    )
    grad_high_far, grad_low_far = swap(grad_high, 0, 1), swap(grad_low, 0, 1)
    down_keep, down = chain(lambda *a: wide_grad(place, 2, *a), *downs, down)
    up, down = swap(up, 2, 0), swap(down, 4, 0)
    grad_high_far, grad_low_far = chain.wait(grad_high_far, grad_low_far)

    own, other = (grad_low, grad_high), (grad_low_far, grad_high_far)
    proj = chain(
        lambda *a: attend_back(place, 1, 1, *a), qkv_far, own, other, w_out_far, tables
    )
    up, down = chain.wait(up, down)
    up_keep, up, down_keep, down = chain(
        lambda *a: add_split(place, (2, 1), *a), up_keep, up, down_keep, down
    )
    up, down = swap(up, 4, 0), swap(down, 2, 0)
    (proj,) = chain(
        lambda *a: attend_back(place, 0, 1, *a), qkv_near, own, other, w_out, tables, proj
    )
    first_dests, second_dests = [(0, 2, 2, 0, 1), (2, 1, 2, 0, 2)], [(0, 1, 2, 1, 2)]
    first, second = chain(
        lambda *a: narrow_grad(place, *a[:3], first_dests), normed, normed_far, proj
    )
    (second,) = chain(
        lambda *a: narrow_grad(place, *a[:3], second_dests, kept=a[3]),
        own,
        other,
        heads[None],
        [second],
    )
    first, second = swap(first, 1, 0), swap(second, 1, 0)
    up, down = chain.wait(up, down)
    wide_near, wide_far = run(add_last, up_keep, up, down_keep, down)
    wide_far = swap(wide_far, 0, 2)
    stay_one = chain(lambda *a: back_rows(place, False, *a), proj, w_qkv, w_qkv_far)
    first, second = chain.wait(first, second)
    first_keep, first, *kept = chain(
        lambda *a: narrow_grad(place, *a[:3], first_dests, a[3]),
        normed,
        normed_far,
        proj,
        [first, second],
    )
    second_keep, second = chain(
        lambda *a: narrow_grad(place, *a[:3], second_dests, a[3], a[4]),
        own,
        other,
        heads[None],
        [second],
        kept,
    )
    first, second = swap(first, 2, 0), swap(second, 4, 0)
    leave_one = chain(lambda *a: back_rows(place, True, *a), proj, w_qkv, w_qkv_far)
    back_one = swap(leave_one, 0, 1)
    out_high_leave, out_low_leave, out_high, out_low = run(
        down_rows, hidden_near, hidden_far, w_down, far_pair, resid_high, resid_low
    )
    out_high_far, out_low_far = swap(out_high_leave, 0, 1), swap(out_low_leave, 0, 1)

    def gather(near, arrived):
        piece = run(add_pair, near, arrived)
        for bit in range(3, bits):
            size = piece.shape[1] // 2
            side = (dp_at >> bit) & 1
            mine = lax.dynamic_slice_in_dim(piece, side * size, size, 1)
            theirs = lax.dynamic_slice_in_dim(piece, (1 - side) * size, size, 1)
            piece = add_pair(place, mine, swap(theirs, 1 << bit, 0))
        return lax.all_gather(piece, "dp", axis=0, tiled=False)

    def order_table(order):
        order = order + list(range(3, bits))
        return [
            sum(((j >> (bits - 1 - i)) & 1) << bit for i, bit in enumerate(order))
            for j in range(dp_size)
        ]

    first_keep, first, second_keep, second = chain(
        lambda *a: add_split(place, (2, 1), *a), first_keep, first, second_keep, second
    )
    first, second = swap(first, 4, 0), swap(second, 2, 0)
    wide_all = gather(wide_near, wide_far)
    heads_near, heads_far = run(add_last, first_keep, first, second_keep, second)
    heads_far = swap(heads_far, 0, 2)
    grad_tokens, gain_sum, shift_sum = run(
        first_back, tokens, stay_one, back_one, wide_low, wide_high, gain_one
    )
    sums = chain(
        lambda *a: jnp.concatenate(a, axis=0),
        gain_sum,
        shift_sum,
        gain_low + gain_high,
        shift_low + shift_high,
    )
    steps = [(0, 2), (0, 1)] + [(1 << b, 0) for b in range(bits)]
    sums = chain(lambda a, b: a + b, sums, swap(sums, *steps.pop()))
    heads_all = gather(heads_near, heads_far)
    while steps:
        sums = chain(lambda a, b: a + b, sums, swap(sums, *steps.pop()))
    layer_out = run(layer_rows, out_low, out_high, out_low_far, out_high_far)
    xy, yx = order_table([0, 1, 2]), order_table([0, 2, 1])
    table = jnp.asarray(xy + yx, jnp.int32)
    grad_up, grad_down = chain(lambda v: assemble(table, v), wide_all)
    grad_qkv, grad_out = chain(lambda v: assemble_heads(table, v), heads_all)
    return (
        layer_out,
        grad_tokens,
        sums[0],
        sums[1],
        grad_qkv,
        grad_out,
        sums[2],
        sums[3],
        grad_up,
        grad_down,
    )


def solution(mesh):
    rows = P(AXES, None)
    params = (P(), P(), P(None, None, "tensor"), P("tensor", None))
    wide = (P(None, "tensor"), P("tensor", None))
    return jax.shard_map(
        shards,
        mesh=mesh,
        in_specs=(rows, P("dp")) + params + (P(), P()) + wide + (rows,),
        out_specs=(rows, rows) + params + (P(), P()) + wide,
        check_vma=False,
    )
```

```python
import functools
import math

import jax
import jax.numpy as jnp
import numpy as np
from jax import lax
from jax.experimental import pallas as pl
from jax.experimental.pallas import tpu as pltpu
from jax.sharding import PartitionSpec as P

HD = 128
FF = 6144
EPS = 1e-05
AXES = ("dp", "tensor")
BF = jnp.bfloat16
F32 = jnp.float32
LOG2E = 1.4426950408889634
LONG = 200_000_000_000
VMEM_LIMIT = 56 * 1024 * 1024
VMEM_SPARE = 10 * 1024 * 1024

ODD, SIDE, LIMIT, NEAR_UNIT, FAR_UNIT = 0, 1, 4, 5, 6

NN = (((1,), (0,)), ((), ()))
NT = (((1,), (1,)), ((), ()))
TN = (((0,), (0,)), ((), ()))


def mm(a, b, dims=NN):
    return lax.dot_general(a, b, dims, preferred_element_type=F32)


def swap(value, dp_bits, tensor_bits):
    dp_size = lax.axis_size("dp")
    tensor_size = lax.axis_size("tensor")
    pairs = [
        (d * tensor_size + t, (d ^ dp_bits) * tensor_size + (t ^ tensor_bits))
        for d in range(dp_size)
        for t in range(tensor_size)
    ]
    return lax.ppermute(value, AXES, pairs)


class Chain:
    def __init__(self):
        self.last = None

    def __call__(self, call, *args):
        if self.last is not None:
            leaves, tree = jax.tree.flatten(args)
            leaves = lax.optimization_barrier(tuple(leaves) + (self.last,))[:-1]
            args = jax.tree.unflatten(tree, leaves)
        out = call(*args)
        self.last = jax.tree.leaves(out)[0]
        return out

    def wait(self, *args):
        return self(lambda *v: v[0] if len(v) == 1 else v, *args)


def dp_piece(weight):
    rows = weight.shape[0] // lax.axis_size("dp")
    return lax.dynamic_slice_in_dim(weight, lax.axis_index("dp") * rows, rows, 0)


def from_all(piece):
    return lax.all_gather(piece, "dp", axis=0, tiled=True)


def stacked_from_all(piece):
    whole = lax.all_gather(piece, "dp", axis=0, tiled=False)
    if piece.shape[1] % 16 == 0:
        return whole
    return whole.transpose(1, 0, 2, 3).reshape(1, 2, -1, piece.shape[2])


def block(shape, index=None):
    if index is None:
        return pl.BlockSpec(shape, lambda *_: (0,) * len(shape))
    return pl.BlockSpec(shape, index)


def shape_of(shape, kind=BF):
    return jax.ShapeDtypeStruct(shape, kind)


def kernel(body, grid, ins, outs, shapes, scratch=(), aliases=None, cost=1):
    def call(place, *args):
        pairs = list(zip(ins, args)) + list(zip(jax.tree.leaves(outs), jax.tree.leaves(shapes)))
        blocks = [
            2 * math.prod(spec.block_shape) * array.dtype.itemsize
            for spec, array in pairs
            if spec.block_shape is not None
        ]
        blocks += [math.prod(one.shape) * jnp.dtype(one.dtype).itemsize for one in scratch]
        return pl.pallas_call(
            body,
            grid_spec=pltpu.PrefetchScalarGridSpec(
                num_scalar_prefetch=1,
                grid=grid,
                in_specs=ins,
                out_specs=outs,
                scratch_shapes=list(scratch),
            ),
            out_shape=shapes,
            input_output_aliases=aliases or {},
            compiler_params=pltpu.CompilerParams(
                vmem_limit_bytes=min(VMEM_LIMIT, sum(blocks) + VMEM_SPARE)
            ),
            cost_estimate=pl.CostEstimate(flops=cost, bytes_accessed=1, transcendentals=0),
        )(place, *args)

    return call


def rows_at(start, size):
    return pl.ds(pl.multiple_of(start, size), size)


def norm_stats(values):
    center = values - jnp.mean(values, axis=-1, keepdims=True)
    spread = jnp.mean(center * center, axis=-1, keepdims=True)
    inverse = lax.rsqrt(spread + EPS)
    return center * inverse, inverse


def norm_back(grads, normal, inverse, gain):
    scaled = grads * gain
    mean_one = jnp.mean(scaled, axis=-1, keepdims=True)
    mean_two = jnp.mean(scaled * normal, axis=-1, keepdims=True)
    return (
        inverse * (scaled - mean_one - normal * mean_two),
        jnp.sum(grads * normal, axis=0, keepdims=True),
        jnp.sum(grads, axis=0, keepdims=True),
    )


def first_norm(place, tokens, gain, shift):
    rows, depth = tokens.shape
    half = rows // 2

    def body(_, x, gain, shift, low, high):
        normal, _ = norm_stats(x[...].astype(F32))
        value = (normal * gain[...] + shift[...]).astype(BF)
        pl.when(pl.program_id(0) == 0)(lambda: low.__setitem__(..., value))
        pl.when(pl.program_id(0) == 1)(lambda: high.__setitem__(..., value))

    return kernel(
        body,
        (2,),
        [block((half, depth), lambda i, _: (i, 0))] + [block((1, depth))] * 2,
        [block((half, depth))] * 2,
        [shape_of((half, depth))] * 2,
    )(place, tokens, gain, shift)


def rope_tables(length):
    frequency = np.exp(
        np.arange(HD // 2, dtype=np.float32) * np.float32(-2.0 * math.log(10000.0) / HD)
    ).astype(np.float32)
    angles = (np.arange(length, dtype=np.float32)[:, None] * frequency[None, :]).astype(np.float64)
    cos_part, sin_part = np.cos(angles), np.sin(angles)
    return (
        np.concatenate([cos_part, cos_part], axis=1).astype(np.float32),
        np.concatenate([-sin_part, sin_part], axis=1).astype(np.float32),
    )


def project(place, own, other, weight, tables, through=None):
    part, depth = own[0].shape
    width = weight.shape[2]

    def body(p, ol, oh, tl, th, weight, cos, sin, *refs):
        out = refs[-1]
        if through is not None:
            out = refs[1]
            pl.when(pl.program_id(0) < 2)(lambda: refs[2].__setitem__(..., refs[0][...]))
            pl.when(pl.program_id(0) >= 2)(lambda: refs[3].__setitem__(..., refs[0][...]))

        def go(source):
            x = source[...]
            for c in range(3):
                result = mm(x, weight[c])
                if c == 2:
                    out[c] = result.astype(BF)
                    continue
                for h in range(width // HD):
                    one = result[:, h * HD : (h + 1) * HD]
                    turned = one * cos[...] + pltpu.roll(one, HD // 2, 1) * sin[...]
                    out[c, :, h * HD : (h + 1) * HD] = turned.astype(BF)

        step = pl.program_id(0)
        at = jnp.where(step // 2 == p[ODD], 0, 2) + step % 2
        for i, source in enumerate((ol, oh, tl, th)):
            pl.when(at == i)(functools.partial(go, source))

    table = block((part, HD), lambda i, _: (i, 0))
    size = part // 2
    ins, outs = [], []
    if through is not None:
        ins = [block((size, depth), lambda i, _: (i, 0))]
        outs = [
            block((size, depth), lambda i, _: (jnp.minimum(i, 1), 0)),
            block((size, depth), lambda i, _: (jnp.maximum(i - 2, 0), 0)),
        ]
    return kernel(
        body,
        (4,),
        [block((part, depth))] * 4 + [block((3, depth, width)), table, table] + ins,
        [block((3, part, width), lambda i, _: (0, i, 0))] + outs,
        [shape_of((3, 4 * part, width))] + [shape_of((part, depth))] * len(outs),
    )(place, *own, *other, weight, *tables, *([through] if ins else []))


QB = 256


EXP_SCALE = HD ** (-0.5) * LOG2E


def masked(scores):
    key_at = lax.broadcasted_iota(jnp.int32, scores.shape, 0)
    row_at = lax.broadcasted_iota(jnp.int32, scores.shape, 1)
    return jnp.where(key_at <= row_at, scores, -1e30)


def probs_t(q, k_ref, first):
    diagonal = masked(mm(k_ref[0, first : first + QB], q, NT))
    top = jnp.max(diagonal, axis=0, keepdims=True)
    before = None
    if first:
        before = mm(k_ref[0, :first], q, NT)
        top = jnp.maximum(top, jnp.max(before, axis=0, keepdims=True))
    diagonal = jnp.exp2((diagonal - top) * EXP_SCALE)
    total = jnp.sum(diagonal, axis=0, keepdims=True)
    if first:
        before = jnp.exp2((before - top) * EXP_SCALE)
        total = total + jnp.sum(before, axis=0, keepdims=True)
    return before, diagonal, 1.0 / total


def attend(place, far, qkv, kept=()):
    _, length, width = qkv.shape
    heads = width // HD

    def body(_, q_ref, k_ref, v_ref, *refs):
        out_ref = refs[-1]
        for first in range(0, length, QB):
            last = first + QB
            before, diagonal, inverse = probs_t(q_ref[0, first:last], k_ref, first)
            blended = mm(v_ref[0, first:last], diagonal.astype(BF), TN)
            if first:
                blended = blended + mm(v_ref[0, :first], before.astype(BF), TN)
            out_ref[first:last, :] = (blended * inverse).T.astype(BF)

    spec = lambda c: block((1, length, HD), lambda h, _: (c, 0, h))
    return kernel(
        body,
        (heads,),
        [spec(0), spec(1), spec(2)] + [pl.BlockSpec(memory_space=pl.ANY)] * len(kept),
        [block((length, HD), lambda h, _: (0, h + heads * far))],
        [shape_of((length, 2 * width))],
        aliases={4 + i: i for i in range(len(kept))},
    )(place, qkv, qkv, qkv, *kept)


def attend_back(place, far, cost, qkv, own, other, w_out, tables, kept=()):
    _, length, width = qkv.shape
    heads = width // HD
    depth = w_out.shape[1]
    part = length // 4

    def unturn(grads, cos, sin):
        return (grads * cos - pltpu.roll(grads, HD // 2, 1) * sin).astype(BF)

    def body(p, q_ref, k_ref, v_ref, ol, oh, tl, th, w_ref, cos, sin, *refs):
        out, g_ref, dk_ref, dv_ref = refs[-4:]
        for base, low, high in ((p[ODD] * 2, ol, oh), ((1 - p[ODD]) * 2, tl, th)):
            g_ref[rows_at(base * part, part)] = mm(low[...], w_ref[...], NT).astype(BF)
            g_ref[rows_at((base + 1) * part, part)] = mm(high[...], w_ref[...], NT).astype(BF)
        for first in reversed(range(0, length, QB)):
            last = first + QB
            q = q_ref[0, first:last]
            g = g_ref[first:last]
            *weights, inverse = probs_t(q, k_ref, first)
            parts = []
            inner = 0.0
            for weight, here in zip(weights, (slice(0, first), slice(first, last))):
                if weight is None:
                    continue
                grad_probs = mm(v_ref[0, here], g, NT)
                inner = inner + jnp.sum(weight * grad_probs, axis=0, keepdims=True)
                parts.append((here, weight, grad_probs))
            inner = inner * inverse
            scaled = inverse * HD ** (-0.5)
            grad_q = 0.0
            for here, weight, grad_probs in parts:
                grad_scores = (weight * ((grad_probs - inner) * scaled)).astype(BF)
                grad_v = mm((weight * inverse).astype(BF), g)
                grad_k = mm(grad_scores, q)
                if last == length:
                    dv_ref[here] = grad_v
                    dk_ref[here] = grad_k
                else:
                    dv_ref[here] += grad_v
                    dk_ref[here] += grad_k
                grad_q = grad_q + mm(grad_scores, k_ref[0, here], TN)
            out[0, first:last] = unturn(grad_q, cos[first:last], sin[first:last])
        out[1] = unturn(dk_ref[...], cos[...], sin[...])
        out[2] = dv_ref[...].astype(BF)

    spec = lambda c: block((1, length, HD), lambda h, _: (c, 0, h))
    piece = block((part, depth))
    table = block((length, HD))
    return kernel(
        body,
        (heads,),
        [spec(0), spec(1), spec(2)]
        + [piece] * 4
        + [block((HD, depth), lambda h, _: (h, 0)), table, table]
        + [pl.BlockSpec(memory_space=pl.ANY)] * len(kept),
        [block((3, length, HD), lambda h, _: (0, 0, h + heads * far))],
        [shape_of((3, length, 2 * width))],
        [pltpu.VMEM((length, HD), BF), pltpu.VMEM((length, HD), F32), pltpu.VMEM((length, HD), F32)],
        {11 + i: i for i in range(len(kept))},
        cost,
    )(place, qkv, qkv, qkv, *own, *other, w_out, *tables, *kept)


def head_rows(place, leave, heads, w_near, w_far):
    length, width = heads.shape
    depth = w_near.shape[1]
    half = length // 4
    kind = BF if leave else F32
    cols = depth // 2

    def body(_, heads, w_near, w_far, low, high):
        total = mm(heads[...], jnp.concatenate([w_near[...], w_far[...]], axis=0))
        low[...] = total[:half].astype(kind)
        high[...] = total[half:].astype(kind)

    weight = block((width // 2, cols), lambda i, p: (0, i))
    return kernel(
        body,
        (2,),
        [
            block((2 * half, width), lambda i, p: (1 - p[ODD] if leave else p[ODD], 0)),
            weight,
            weight,
        ],
        [block((half, cols), lambda i, p: (0, i))] * 2,
        [shape_of((half, depth), kind)] * 2,
    )(place, heads, w_near, w_far)


def second_norm(place, which, stay, tokens, arrived, gain, shift):
    half, depth = stay.shape
    size = half // 2

    def body(_, stay, tokens, arrived, gain, shift, normed, resid):
        total = tokens[...].astype(F32) + stay[...] + arrived[...].astype(F32)
        resid[...] = total
        normal, _ = norm_stats(total)
        normed[...] = (normal * gain[...] + shift[...]).astype(BF)

    piece = block((size, depth), lambda i, _: (i, 0))
    return kernel(
        body,
        (2,),
        [piece, block((size, depth), lambda i, _: (2 * which + i, 0)), piece]
        + [block((1, depth))] * 2,
        [piece] * 2,
        [shape_of((half, depth)), shape_of((half, depth), F32)],
    )(place, stay, tokens, arrived, gain, shift)


def gelu_pair(v):
    c = math.sqrt(2.0 / math.pi)
    square = v * v
    t = jnp.tanh(v * (c + (c * 0.044715) * square))
    half = 0.5 + 0.5 * t
    slope = half + v * (0.5 - 0.5 * t * t) * (c + (3.0 * 0.044715 * c) * square)
    return v * half, slope


UB = 768
SB = 256


def hidden_grads(place, cost, rows_in, weight):
    each, depth = rows_in[0].shape
    count = each * len(rows_in)
    parts, _, rows, _ = weight.shape
    units = parts * rows
    step = UB // rows if rows < UB else 1
    tile = (step, 1, min(rows, UB), depth)
    last = weight.shape[1] - 1

    def body(_, *refs):
        *sources, weight, out = refs
        w = weight[:, 0].reshape(UB, depth)
        for i, source in enumerate(sources):
            out[i * each : (i + 1) * each] = mm(source[...], w, NT).astype(BF)

    place_of = lambda j: (j, last, 0, 0) if rows <= UB else (0, last, j, 0)
    return kernel(
        body,
        (units // UB,),
        [block((each, depth))] * len(rows_in) + [block(tile, lambda j, _: place_of(j))],
        block((count, UB), lambda j, _: (0, j)),
        shape_of((count, units)),
        cost=cost,
    )(place, *rows_in, weight)


def feed(group, place, normed, normed_far, cot, cot_far, w_up, far_pair, hidden_grad, kept=()):
    half, depth = normed.shape
    size = 2 * half
    units = w_up.shape[1]
    near_steps = units // UB
    far_parts, _, far_rows, _ = far_pair.shape

    def body(p, own, other, g_own, g_other, un, uf, gno, gnt, gfo, gft, *refs):
        hn, pn, hf, pf, rows, grads, stay, leave, total = refs[-9:]
        step = pl.program_id(0)

        @pl.when(step == 0)
        def _():
            total[...] = jnp.zeros_like(total)
            rows[:half] = own[...]
            rows[half:] = other[...]
            grads[:half] = g_own[...]
            grads[half:] = g_other[...]

        def work(up, grad_own, grad_other, hidden, pre):
            for at in range(0, UB, SB):
                there = slice(at, at + SB)
                value, slope = gelu_pair(mm(rows[...], up[:, there]))
                hidden[:, there] = value.astype(BF)
                pre[:half, there] = (grad_own[:, there].astype(F32) * slope[:half]).astype(BF)
                pre[half:, there] = (grad_other[:, there].astype(F32) * slope[half:]).astype(BF)
            total[...] += mm(pre[...], up, NT)

        def part(first_unit, up, grad_own, grad_other, hidden, pre):
            live = first_unit < p[LIMIT]

            @pl.when(live)
            def _():
                work(up(), grad_own, grad_other, hidden, pre)

            @pl.when(jnp.logical_not(live))
            def _():
                hidden[...] = jnp.zeros((size, UB), BF)
                pre[...] = jnp.zeros((size, UB), BF)

        @pl.when(step < near_steps)
        def _():
            part(p[NEAR_UNIT] + step * UB, lambda: un[...], gno, gnt, hn, pn)

        @pl.when(step >= near_steps)
        def _():
            far_up = lambda: uf[:, 0].reshape(depth, UB)
            part(p[FAR_UNIT] + (step - near_steps) * UB, far_up, gfo, gft, hf, pf)

        @pl.when(step == 2 * near_steps - 1)
        def _():
            stay[...] = total[:half]
            leave[...] = total[half:].astype(BF)

    near = lambda j: jnp.minimum(j, near_steps - 1)
    far = lambda j: jnp.maximum(j - near_steps, 0)
    wide = [block((size, UB), lambda j, _, at=at: (group, at(j))) for at in (near, far)]
    slim = [block((half, UB), lambda j, _, at=at: (1 - group, at(j))) for at in (near, far)]
    piece = block((half, depth))
    rows = block((size, depth), lambda j, _: (group, 0))
    return kernel(
        body,
        (2 * near_steps,),
        [piece, piece, block((half, depth), lambda j, _: (1 - group, 0)), piece]
        + [block((depth, UB), lambda j, _: (0, near(j)))]
        + [block((far_parts, 1, far_rows, UB), lambda j, _: (0, 0, 0, far(j)))]
        + [slim[0], slim[0], slim[1], slim[1]]
        + [pl.BlockSpec(memory_space=pl.ANY)] * len(kept),
        [wide[0], wide[0], wide[1], wide[1], rows, rows, piece, piece],
        [shape_of((2 * size, units))] * 4
        + [shape_of((2 * size, depth))] * 2
        + [shape_of((half, depth), F32), shape_of((half, depth))],
        [pltpu.VMEM((size, depth), F32)],
        {11 + i: i for i in range(len(kept))},
    )(place, normed, normed_far, cot, cot_far, w_up, far_pair, *hidden_grad, *kept)


def second_back(place, which, resid, stay, arrived, cot, gain):
    half, depth = resid.shape
    size = half // 2

    def body(_, resid, stay, arrived, cot, gain, low, wide, gain_sum, shift_sum):
        normal, inverse = norm_stats(resid[...])
        grad, gains, shifts = norm_back(
            stay[...] + arrived[...].astype(F32), normal, inverse, gain[...]
        )
        grad = grad + cot[...].astype(F32)
        wide[...] = grad
        low[...] = grad.astype(BF)

        @pl.when(pl.program_id(0) == 0)
        def _():
            gain_sum[...] = gains
            shift_sum[...] = shifts

        @pl.when(pl.program_id(0) > 0)
        def _():
            gain_sum[...] += gains
            shift_sum[...] += shifts

    piece = block((size, depth), lambda i, _: (i, 0))
    vector = block((1, depth))
    return kernel(
        body,
        (2,),
        [piece] * 3 + [block((size, depth), lambda i, _: (2 * which + i, 0)), vector],
        [piece, piece, vector, vector],
        [shape_of((half, depth)), shape_of((half, depth), F32)] + [shape_of((1, depth), F32)] * 2,
    )(place, resid, stay, arrived, cot, gain)


def down_rows(place, near, far, w_near, far_pair, resid_high, resid_low):
    rows, units = near.shape
    depth = w_near.shape[1]
    half = rows // 4
    cols = depth // 3
    far_parts, _, far_rows, _ = far_pair.shape

    def body(_, near, far, w_near, w_far, resid_high, resid_low, high, low, out_high, out_low):
        w_second = w_far[:, 0].reshape(units, cols)
        for i, (stay, resid, leave) in enumerate(
            ((out_high, resid_high, high), (out_low, resid_low, low))
        ):
            here = slice(2 * i * half, 2 * (i + 1) * half)
            total = mm(near[here], w_near[...]) + mm(far[here], w_second)
            stay[...] = total[:half] + resid[...]
            leave[...] = total[half:].astype(BF)

    hidden = block((rows, units))
    piece = block((half, cols), lambda j, _: (0, j))
    return kernel(
        body,
        (3,),
        [
            hidden,
            hidden,
            block((units, cols), lambda j, _: (0, j)),
            block((far_parts, 1, far_rows, cols), lambda j, _: (0, 1, 0, j)),
            piece,
            piece,
        ],
        [piece] * 4,
        [shape_of((half, depth))] * 2 + [shape_of((half, depth), F32)] * 2,
        cost=LONG,
    )(place, near, far, w_near, far_pair, resid_high, resid_low)


def layer_rows(place, out_low, out_high, low, high):
    half, depth = low.shape

    def body(_, out_low, out_high, low, high, out):
        out[:half] = (out_low[...] + low[...].astype(F32)).astype(BF)
        out[half:] = (out_high[...] + high[...].astype(F32)).astype(BF)

    piece = block((half, depth))
    return kernel(body, (1,), [piece] * 4, block((2 * half, depth)), shape_of((2 * half, depth)))(
        place, out_low, out_high, low, high
    )


def wide_grad(place, bit, lefts, rights, arrived=None):
    rows, width = lefts[0].shape
    depth = rights[0].shape[1]
    half = width // 2
    cols = depth // 2
    last = arrived is not None

    def body(p, l0, l1, r0, r1, *refs):
        turned = refs[-1]
        shard = pl.program_id(0)

        @pl.when(pl.program_id(1) == 0)
        def _():
            pl.when(shard == 0)(lambda: turned.__setitem__(..., l0[...].T))
            pl.when(shard == 1)(lambda: turned.__setitem__(..., l1[...].T))

        def go(right):
            if not last:
                refs[0][0, 0] = mm(turned[...], right[...]).astype(BF)
                return
            for out, side in ((refs[1], p[SIDE + bit]), (refs[2], 1 - p[SIDE + bit])):
                here = rows_at(side * (half // 2), half // 2)
                value = mm(turned[here], right[...]) + refs[0][0, 0, here].astype(F32)
                out[0, 0] = value.astype(BF)

        pl.when(shard == 0)(lambda: go(r0))
        pl.when(shard == 1)(lambda: go(r1))

    side = lambda p: p[SIDE] if last else 1 - p[SIDE]
    left = block((rows, half), lambda s, j, p: (0, side(p)))
    right = lambda shard: block(
        (rows, cols), lambda s, j, p: (0, jnp.where(s == shard, j, 1 - shard))
    )
    tall = lambda size: block((1, 1, size, cols), lambda s, j, p: (s, 0, 0, j))
    if last:
        outs = [tall(half // 2)] * 2
        shapes = [shape_of((2, 1, half // 2, depth))] * 2
    else:
        outs, shapes = tall(half), shape_of((2, 1, half, depth))
    return kernel(
        body,
        (2, 2),
        [left, left, right(0), right(1)] + [tall(half)] * last,
        outs,
        shapes,
        [pltpu.VMEM((half, rows), BF)],
    )(place, *lefts, *rights, *([arrived] if last else []))


def narrow_grad(place, own, other, rights, dests, arrived=(), kept=()):
    rows, depth = own[0].shape
    parts = len(own)
    count, length, width = rights.shape
    half = depth // 2
    last = len(arrived) > 0
    n_out = 2 if last else 1
    size = half // 2 if last else half

    def body(p, *refs):
        own, other, right = refs[:parts], refs[parts : 2 * parts], refs[2 * parts]
        got = refs[2 * parts + 1 : 2 * parts + 1 + len(arrived)]
        outs, turned = refs[-1 - n_out * len(dests) : -1], refs[-1]
        c = pl.program_id(0)

        @pl.when(c == 0)
        def _():
            for lefts, base in ((own, p[ODD]), (other, 1 - p[ODD])):
                for i, left in enumerate(lefts):
                    turned[:, rows_at((base * parts + i) * rows, rows)] = left[...].T

        def go(i, bit):
            if not last:
                value = mm(turned[...], right[0]).astype(BF)
                outs[i][0, 0] = value[:, : width // 2]
                outs[i][1, 0] = value[:, width // 2 :]
                return
            for out, side in ((outs[2 * i], p[SIDE + bit]), (outs[2 * i + 1], 1 - p[SIDE + bit])):
                here = rows_at(side * size, size)
                value = mm(turned[here], right[0])
                for shard in range(2):
                    there = slice(shard * width // 2, (shard + 1) * width // 2)
                    out[shard, 0] = (value[:, there] + got[i][shard, 0, here].astype(F32)).astype(BF)

        for i, (first, many, _, _, bit) in enumerate(dests):
            pl.when((c >= first) & (c < first + many))(functools.partial(go, i, bit))

    side = lambda p: p[SIDE] if last else 1 - p[SIDE]
    left = block((rows, half), lambda c, p: (0, side(p)))

    def tall(dest, size):
        first, many, _, at, _ = dest
        return block(
            (2, 1, size, width // 2), lambda c, p: (0, at + jnp.clip(c - first, 0, many - 1), 0, 0)
        )

    ins = [left] * (2 * parts) + [block((1, length, width), lambda c, p: (c, 0, 0))]
    ins += [tall(dest, half) for dest in dests] * last
    return kernel(
        body,
        (count,),
        ins + [pl.BlockSpec(memory_space=pl.ANY)] * len(kept),
        [tall(dest, size) for dest in dests for _ in range(n_out)],
        [shape_of((2, dest[2], size, width // 2)) for dest in dests for _ in range(n_out)],
        [pltpu.VMEM((half, length), BF)],
        {1 + len(ins) + i: i for i in range(len(kept))},
    )(place, *own, *other, rights, *arrived, *kept)


def add_split(place, bits, *pairs):
    _, count, rows, width = pairs[0].shape
    half = rows // 2

    def body(p, *refs):
        for i, bit in enumerate(bits):
            mine, theirs = refs[2 * i : 2 * i + 2]
            outs = refs[2 * (len(bits) + i) : 2 * (len(bits) + i) + 2]
            for out, side in zip(outs, (p[SIDE + bit], 1 - p[SIDE + bit])):
                here = rows_at(side * half, half)
                out[0, 0] = (mine[0, 0, here].astype(F32) + theirs[0, 0, here].astype(F32)).astype(BF)

    full = block((1, 1, rows, width), lambda s, c, p: (s, c, 0, 0))
    out = block((1, 1, half, width), lambda s, c, p: (s, c, 0, 0))
    n = 2 * len(bits)
    return kernel(
        body, (2, count), [full] * n, [out] * n, [shape_of((2, count, half, width))] * n
    )(place, *pairs)


def add_last(place, *pairs):
    _, count, rows, width = pairs[0].shape
    n = len(pairs) // 2

    def body(_, *refs):
        near, far = refs[-2:]
        for i in range(n):
            for shard, out in ((0, near), (1, far)):
                for c in range(count):
                    mine, theirs = refs[2 * i][shard, c], refs[2 * i + 1][shard, c]
                    out[i * count + c] = (mine.astype(F32) + theirs.astype(F32)).astype(BF)

    full = block((2, count, rows, width))
    out = block((n * count, rows, width))
    return kernel(
        body, (1,), [full] * (2 * n), [out, out], [shape_of((n * count, rows, width))] * 2
    )(place, *pairs)


def add_pair(place, near, arrived):
    shape = near.shape

    def body(_, mine, theirs, out):
        out[...] = (mine[...].astype(F32) + theirs[...].astype(F32)).astype(BF)

    full = block(shape)
    return kernel(body, (1,), [full, full], full, shape_of(shape))(place, near, arrived)


def assemble(table, whole):
    size, _, rows, width = whole.shape

    def body(_, one, two, out_one, out_two):
        out_one[...] = one[0, 0].astype(F32)
        out_two[...] = two[0, 0].astype(F32)

    piece = lambda i: block((1, 1, rows, width), lambda j, t: (t[size * i + j], i, 0, 0))
    return kernel(
        body,
        (size,),
        [piece(0), piece(1)],
        [block((rows, width), lambda j, t: (j, 0))] * 2,
        [shape_of((rows * size, width), F32)] * 2,
    )(table, whole, whole)


def assemble_heads(table, whole):
    size, count, rows, width = whole.shape
    group = 2 if 2 * rows % 128 == 0 else size

    def body(_, *refs):
        pieces, (out, last) = refs[:-2], refs[-2:]
        for i in range(group):
            here = slice(i * rows, (i + 1) * rows)
            one, two = pieces[2 * i : 2 * i + 2]
            out[:2, here] = one[0].astype(F32)
            out[2, here] = two[0, 0].astype(F32)
        turned = jnp.concatenate([pieces[2 * i + 1][0, 1] for i in range(group)], axis=0)
        last[...] = turned.astype(F32).T

    piece = lambda i, k: block(
        (1, 2, rows, width), lambda j, t: (t[size * k + group * j + i], k, 0, 0)
    )
    return kernel(
        body,
        (size // group,),
        [piece(i, k) for i in range(group) for k in range(2)],
        [
            block((count - 1, group * rows, width), lambda j, t: (0, j, 0)),
            block((width, group * rows), lambda j, t: (0, j)),
        ],
        [shape_of((count - 1, rows * size, width), F32), shape_of((width, rows * size), F32)],
    )(table, *([whole] * (2 * group)))


def back_rows(place, leave, proj, w_near, w_far):
    count, length, width = proj.shape
    depth = w_near.shape[1]
    rows = length // 2
    cols = depth // 3
    kind = BF if leave else F32

    def body(_, proj, w_near, w_far, out):
        total = 0.0
        for c in range(count):
            weight = jnp.concatenate([w_near[c], w_far[c]], axis=1)
            total = total + mm(proj[c], weight, NT)
        out[...] = total.astype(kind)

    weight = block((count, cols, width // 2), lambda j, p: (0, j, 0))
    return kernel(
        body,
        (3,),
        [
            block((count, rows, width), lambda j, p: (0, 1 - p[ODD] if leave else p[ODD], 0)),
            weight,
            weight,
        ],
        block((rows, cols), lambda j, p: (0, j)),
        shape_of((rows, depth), kind),
        cost=LONG,
    )(place, proj, w_near, w_far)


def first_back(place, tokens, stay, arrived, resid_low, resid_high, gain):
    rows, depth = tokens.shape
    half = rows // 2

    def body(_, tokens, stay, arrived, resid_low, resid_high, gain, out, gain_sum, shift_sum):
        normal, inverse = norm_stats(tokens[...].astype(F32))
        grad, gains, shifts = norm_back(
            stay[...] + arrived[...].astype(F32), normal, inverse, gain[...]
        )

        @pl.when(pl.program_id(0) == 0)
        def _():
            out[...] = grad + resid_low[...]
            gain_sum[...] = gains
            shift_sum[...] = shifts

        @pl.when(pl.program_id(0) == 1)
        def _():
            out[...] = grad + resid_high[...]
            gain_sum[...] += gains
            shift_sum[...] += shifts

    tile = block((half, depth), lambda i, _: (i, 0))
    piece = block((half, depth))
    vector = block((1, depth))
    return kernel(
        body,
        (2,),
        [tile, tile, tile, piece, piece, vector],
        [tile, vector, vector],
        [shape_of((rows, depth), F32)] + [shape_of((1, depth), F32)] * 2,
        cost=LONG,
    )(place, tokens, stay, arrived, resid_low, resid_high, gain)


def shards(
    tokens,
    granularity,
    gain_one,
    shift_one,
    w_qkv,
    w_out,
    gain_two,
    shift_two,
    w_up,
    w_down,
    cotangent,
):
    tensor_size = lax.axis_size("tensor")
    dp_size = lax.axis_size("dp")
    rank = lax.axis_index("tensor")
    dp_at = lax.axis_index("dp")
    local_rows, depth = tokens.shape
    seq_len = local_rows * tensor_size // granularity.shape[0]
    assert tensor_size == 4 and seq_len == 2 * local_rows and dp_size % 8 == 0
    half = local_rows // 2
    hidden_here = w_up.shape[1]
    head_width = w_qkv.shape[2]
    bits = dp_size.bit_length() - 1
    tables = [jnp.asarray(t) for t in rope_tables(seq_len)]
    gain_one, shift_one, gain_two, shift_two = (
        v[None, :] for v in (gain_one, shift_one, gain_two, shift_two)
    )
    limits = jnp.left_shift(jnp.ones_like(granularity), granularity) * (FF // 8)
    upper = rank // 2
    place = jnp.stack(
        [
            rank % 2,
            dp_at & 1,
            (dp_at >> 1) & 1,
            (dp_at >> 2) & 1,
            jnp.where(upper == 0, limits[0], limits[1]),
            rank * hidden_here,
            (rank ^ 2) * hidden_here,
        ]
    ).astype(jnp.int32)
    chain = Chain()
    run = lambda call, *args: chain(functools.partial(call, place), *args)

    piece_qkv = swap(chain(dp_piece, w_qkv.reshape(3 * depth, head_width)), 0, 2)
    normed = run(first_norm, tokens, gain_one, shift_one)
    normed_far = [swap(v, 0, 1) for v in normed]
    w_down_own = w_down[None, None]
    own_near = chain(lambda *a: hidden_grads(place, LONG, *a), [cotangent], w_down_own)
    normed_far[0], piece_qkv = chain.wait(normed_far[0], piece_qkv)
    w_qkv_far = from_all(piece_qkv).reshape(w_qkv.shape)
    piece_out, piece_pair = chain(
        lambda a, b, c: (dp_piece(a), jnp.stack([dp_piece(b), dp_piece(c)])), w_out, w_up, w_down
    )
    piece_out, piece_pair = swap(piece_out, 0, 2), swap(piece_pair, 0, 2)
    normed_far[1], piece_out = chain.wait(normed_far[1], piece_out)
    w_out_far = from_all(piece_out)
    qkv_near, *cot_far = run(project, normed, normed_far, w_qkv, tables, cotangent)
    cot_far = [swap(v, 0, 1) for v in cot_far]
    heads = chain(lambda *a: attend(place, 0, *a), qkv_near)
    (qkv_far,) = run(project, normed, normed_far, w_qkv_far, tables)
    (heads,) = chain(lambda *a: attend(place, 1, *a), qkv_far, heads)
    low, high = chain(lambda *a: head_rows(place, True, *a), heads, w_out, w_out_far)
    high, low = swap(high, 0, 1), swap(low, 0, 1)
    cot_far[1], piece_pair = chain.wait(cot_far[1], piece_pair)
    far_pair = stacked_from_all(piece_pair)
    stay_low, stay_high = chain(lambda *a: head_rows(place, False, *a), heads, w_out, w_out_far)
    norm_args = (gain_two, shift_two)
    normed_high, resid_high = chain(
        lambda *a: second_norm(place, 1, *a), stay_high, tokens, high, *norm_args
    )
    normed_high_far = swap(normed_high, 0, 1)
    other_near = chain(lambda *a: hidden_grads(place, 1, *a), cot_far, w_down_own)
    normed_low, resid_low = chain(
        lambda *a: second_norm(place, 0, *a), stay_low, tokens, low, *norm_args
    )
    normed_low_far = swap(normed_low, 0, 1)
    other_far = chain(lambda *a: hidden_grads(place, 1, *a), cot_far, far_pair)
    own_far = chain(lambda *a: hidden_grads(place, 1, *a), [cotangent], far_pair)

    weights = (w_up, far_pair, (own_near, other_near, own_far, other_far))
    *kept, stay_high, leave_high = chain(
        lambda *a: feed(0, place, *a), normed_high, normed_high_far, cotangent, cot_far[1], *weights
    )
    back_high = swap(leave_high, 0, 1)
    *kept, stay_low, leave_low = chain(
        lambda *a: feed(1, place, *a),
        normed_low,
        normed_low_far,
        cotangent,
        cot_far[0],
        *weights,
        kept,
    )
    back_low = swap(leave_low, 0, 1)
    hidden_near, pre_near, hidden_far, pre_far, rows_two, grad_rows = kept
    ups = ((rows_two, rows_two), (pre_near, pre_far))
    downs = ((hidden_near, hidden_far), (grad_rows, grad_rows))
    grad_high, wide_high, gain_high, shift_high = chain(
        lambda *a: second_back(place, 1, *a), resid_high, stay_high, back_high, cotangent, gain_two
    )
    up = swap(chain(lambda *a: wide_grad(place, None, *a), *ups), 1, 0)
    down = swap(chain(lambda *a: wide_grad(place, None, *a), *downs), 1, 0)
    up_keep, up = chain(lambda *a: wide_grad(place, 1, *a), *ups, up)
    grad_low, wide_low, gain_low, shift_low = chain(
        lambda *a: second_back(place, 0, *a), resid_low, stay_low, back_low, cotangent, gain_two
    )
    grad_high_far, grad_low_far = swap(grad_high, 0, 1), swap(grad_low, 0, 1)
    down_keep, down = chain(lambda *a: wide_grad(place, 2, *a), *downs, down)
    up, down = swap(up, 2, 0), swap(down, 4, 0)
    grad_high_far, grad_low_far = chain.wait(grad_high_far, grad_low_far)

    own, other = (grad_low, grad_high), (grad_low_far, grad_high_far)
    proj = chain(
        lambda *a: attend_back(place, 1, 1, *a), qkv_far, own, other, w_out_far, tables
    )
    up, down = chain.wait(up, down)
    up_keep, up, down_keep, down = chain(
        lambda *a: add_split(place, (2, 1), *a), up_keep, up, down_keep, down
    )
    up, down = swap(up, 4, 0), swap(down, 2, 0)
    (proj,) = chain(
        lambda *a: attend_back(place, 0, 1, *a), qkv_near, own, other, w_out, tables, proj
    )
    first_dests, second_dests = [(0, 2, 2, 0, 1), (2, 1, 2, 0, 2)], [(0, 1, 2, 1, 2)]
    first, second = chain(
        lambda *a: narrow_grad(place, *a[:3], first_dests), normed, normed_far, proj
    )
    (second,) = chain(
        lambda *a: narrow_grad(place, *a[:3], second_dests, kept=a[3]),
        own,
        other,
        heads[None],
        [second],
    )
    first, second = swap(first, 1, 0), swap(second, 1, 0)
    up, down = chain.wait(up, down)
    wide_near, wide_far = run(add_last, up_keep, up, down_keep, down)
    wide_far = swap(wide_far, 0, 2)
    stay_one = chain(lambda *a: back_rows(place, False, *a), proj, w_qkv, w_qkv_far)
    first, second = chain.wait(first, second)
    first_keep, first, *kept = chain(
        lambda *a: narrow_grad(place, *a[:3], first_dests, a[3]),
        normed,
        normed_far,
        proj,
        [first, second],
    )
    second_keep, second = chain(
        lambda *a: narrow_grad(place, *a[:3], second_dests, a[3], a[4]),
        own,
        other,
        heads[None],
        [second],
        kept,
    )
    first, second = swap(first, 2, 0), swap(second, 4, 0)
    leave_one = chain(lambda *a: back_rows(place, True, *a), proj, w_qkv, w_qkv_far)
    back_one = swap(leave_one, 0, 1)
    out_high_leave, out_low_leave, out_high, out_low = run(
        down_rows, hidden_near, hidden_far, w_down, far_pair, resid_high, resid_low
    )
    out_high_far, out_low_far = swap(out_high_leave, 0, 1), swap(out_low_leave, 0, 1)

    def gather(near, arrived):
        piece = run(add_pair, near, arrived)
        for bit in range(3, bits):
            size = piece.shape[1] // 2
            side = (dp_at >> bit) & 1
            mine = lax.dynamic_slice_in_dim(piece, side * size, size, 1)
            theirs = lax.dynamic_slice_in_dim(piece, (1 - side) * size, size, 1)
            piece = add_pair(place, mine, swap(theirs, 1 << bit, 0))
        return lax.all_gather(piece, "dp", axis=0, tiled=False)

    def order_table(order):
        order = order + list(range(3, bits))
        return [
            sum(((j >> (bits - 1 - i)) & 1) << bit for i, bit in enumerate(order))
            for j in range(dp_size)
        ]

    first_keep, first, second_keep, second = chain(
        lambda *a: add_split(place, (2, 1), *a), first_keep, first, second_keep, second
    )
    first, second = swap(first, 4, 0), swap(second, 2, 0)
    wide_all = gather(wide_near, wide_far)
    heads_near, heads_far = run(add_last, first_keep, first, second_keep, second)
    heads_far = swap(heads_far, 0, 2)
    grad_tokens, gain_sum, shift_sum = run(
        first_back, tokens, stay_one, back_one, wide_low, wide_high, gain_one
    )
    sums = chain(
        lambda *a: jnp.concatenate(a, axis=0),
        gain_sum,
        shift_sum,
        gain_low + gain_high,
        shift_low + shift_high,
    )
    steps = [(0, 2), (0, 1)] + [(1 << b, 0) for b in range(bits)]
    sums = chain(lambda a, b: a + b, sums, swap(sums, *steps.pop()))
    heads_all = gather(heads_near, heads_far)
    while steps:
        sums = chain(lambda a, b: a + b, sums, swap(sums, *steps.pop()))
    layer_out = run(layer_rows, out_low, out_high, out_low_far, out_high_far)
    xy, yx = order_table([0, 1, 2]), order_table([0, 2, 1])
    table = jnp.asarray(xy + yx, jnp.int32)
    grad_up, grad_down = chain(lambda v: assemble(table, v), wide_all)
    grad_qkv, grad_out = chain(lambda v: assemble_heads(table, v), heads_all)
    return (
        layer_out,
        grad_tokens,
        sums[0],
        sums[1],
        grad_qkv,
        grad_out,
        sums[2],
        sums[3],
        grad_up,
        grad_down,
    )


def solution(mesh):
    rows = P(AXES, None)
    params = (P(), P(), P(None, None, "tensor"), P("tensor", None))
    wide = (P(None, "tensor"), P("tensor", None))
    return jax.shard_map(
        shards,
        mesh=mesh,
        in_specs=(rows, P("dp")) + params + (P(), P()) + wide + (rows,),
        out_specs=(rows, rows) + params + (P(), P()) + wide,
        check_vma=False,
    )
```
